256 devices in a mesh: ctx: 64 (over z, y, core), head: 4 (over x).
Axes of the slice: x: 4, y: 4, z: 8, core: 2. Of those that a mesh axis runs over, the one named last changes fastest.
Arguments:
- queries: bfloat16 [16384, 32, 128], P('ctx', 'head'), may hold values from -6 to 6
- keys: bfloat16 [16384, 32, 128], P('ctx', 'head'), may hold values from -6 to 6
- values: bfloat16 [16384, 32, 128], P('ctx', 'head'), may hold values from -60 to 60, as said below
- out_grad: bfloat16 [16384, 32, 128], P('ctx', 'head'), may hold values from -6 to 6
- gain: float32 [32, 128], P('head'), may hold values from 0.1 to 1.9
- starts: int32 [4], replicated, may hold values from 0 to 16000, as said below
Outputs:
- query_grad: bfloat16 [16384, 32, 128], P('ctx', 'head')
- key_grad: bfloat16 [16384, 32, 128], P('ctx', 'head')
- value_grad: bfloat16 [16384, 32, 128], P('ctx', 'head')
The draws below stay inside these ranges and needn't reach their ends.
Inputs may be any that keep to these rules, and one draw needn't show every extreme that they name: starts rise; the first is 0; consecutive starts lie at least 384 apart. Each head's values have their own scale.
All inputs are finite; a program needn't handle non-finite values.
Results may differ from the reference program's by a relative error of at most 0.0058.
Values sent between devices are 32-bit elements; how exact they have to be, the bound alone decides.
A program may use at most 128 MiB of HBM per device.

```python
import math
import jax
import jax.numpy as jnp
from jax import lax

HEADS = 32
HEAD_DIM = 128
TOK_DEV = 256
SEGS = 4
TOKENS = 16384
SEG_MIN = 384


def draw_values(key, part):
    key = jax.random.fold_in(key, 7)
    key_scale, key_base = jax.random.split(key, 2)
    rise = 3.0 ** (jnp.arange(HEADS, dtype=jnp.float32) / max(HEADS - 1, 1))
    spread = jnp.exp(jax.random.uniform(key_scale, (HEADS,), minval=0.0, maxval=math.log(4.0)))
    base = jnp.clip(jax.random.normal(key_base, (TOKENS, HEADS, HEAD_DIM)), -5.0, 5.0)
    return (base * (rise * spread)[None, :, None]).astype(jnp.bfloat16)


def draw_starts(key, part):
    key = jax.random.fold_in(key, 11)
    slack = TOKENS - SEGS * SEG_MIN
    extra = jnp.sort(jax.random.randint(key, (SEGS - 1,), 0, slack + 1)).astype(jnp.int32)
    extra = extra.at[SEGS - 2].set(slack)
    later = jnp.arange(1, SEGS, dtype=jnp.int32) * SEG_MIN + extra
    return jnp.concatenate([jnp.zeros((1,), jnp.int32), later]).astype(jnp.int32)


def level_of(key, dims, cuts, low, high):
    level, own = 1.0, jax.random.fold_in(key, 6)
    for position, blocks in cuts:
        draws = jnp.exp(jax.random.uniform(jax.random.fold_in(own, position), (blocks,), jnp.float32, low / len(cuts), high / len(cuts)))
        level = level * jnp.repeat(draws, dims[position] // blocks).reshape([-1 if axis == position else 1 for axis in range(len(dims))])
    return level


def noise(own_key, shape, scale, bound, shards=(), held_as=jnp.bfloat16):
    drawn = jax.random.normal(own_key, shape, jnp.float32) * scale
    if len(shards) > 0:
        drawn = level_of(own_key, shape, shards, -0.22, 0.18) * drawn
    return jnp.clip(drawn, min=-bound, max=bound).astype(held_as)


def setup_inputs(seed: int = 0) -> dict:
    streams_of = jax.random.split(jax.random.key(seed), 7)
    queries = noise(streams_of[0], (TOKENS, HEADS, HEAD_DIM), 1.0, 6.0, ((0, 64), (1, 4)))
    keys = noise(streams_of[1], (TOKENS, HEADS, HEAD_DIM), 1.0, 6.0, ((0, 64), (1, 4)))
    values = draw_values(jax.random.fold_in(streams_of[6], 71), 0)
    out_grad = noise(streams_of[3], (TOKENS, HEADS, HEAD_DIM), 1.0, 6.0, ((0, 64), (1, 4)))
    gain = jnp.clip(1.0 + 0.18 * jax.random.normal(streams_of[4], (HEADS, HEAD_DIM), jnp.float32), 0.1, 1.9)
    starts = draw_starts(jax.random.fold_in(streams_of[6], 71), 0)
    return dict(queries=queries, keys=keys, values=values, out_grad=out_grad, gain=gain, starts=starts)


EPSILON = 1e-06

def positions_layout(starts):
    posits = jnp.arange(TOKENS, dtype=jnp.int32)
    seg = (lax.optimization_barrier(jnp.sum((posits[:, None] >= starts[None, :]).astype(jnp.int32), axis=1)) - 1).astype(jnp.int32)
    begins = jnp.any(posits[:, None] == starts[None, :], axis=1)
    return (seg, begins)

def block_layout(seg, begins):
    count = seg.shape[0]
    rows = jnp.arange(count, dtype=jnp.int32)
    mask = (rows[:, None] >= rows[None, :]) & (seg[:, None] == seg[None, :])
    first = (seg == seg[0]) & jnp.logical_not(begins[0])
    last = seg == seg[count - 1]
    cut = jnp.any(begins).astype(jnp.float32)
    return (mask, first[:, None, None], last[:, None, None], cut)

def reference(queries, keys, values, out_grad, gain, starts):
    f32 = jnp.float32
    nblk = TOKENS // TOK_DEV
    seg, begins = positions_layout(starts)

    def blocks(arr):
        return arr.reshape((nblk, TOK_DEV) + arr.shape[1:])

    def forward(state, block):
        qry, key_blk, val, sg, bg = block
        mask, first, last, cut = block_layout(sg, bg)
        qf, kf, vf = (qry.astype(f32), key_blk.astype(f32), val.astype(f32))
        scores = jnp.einsum('ihd,jhd->hij', qf, kf)
        probs = jnp.where(mask[None], scores, 0.0).astype(jnp.bfloat16)
        state_bf = state.astype(jnp.bfloat16)
        inner = jnp.einsum('hij,jhd->ihd', probs.astype(f32), vf)
        outer = jnp.einsum('ihd,hde->ihe', qf, state_bf.astype(f32))
        attn = inner + jnp.where(first, outer, 0.0)
        tail = jnp.einsum('ihd,ihe->hde', kf * last.astype(f32), vf)
        return (tail + (1.0 - cut) * state, (attn, state_bf))
    zero_state = jnp.zeros((HEADS, HEAD_DIM, HEAD_DIM), f32)
    inputs = (blocks(queries), blocks(keys), blocks(values), blocks(seg), blocks(begins))
    unused, (attn_blocks, key_states) = lax.scan(forward, zero_state, inputs)
    attn = attn_blocks.reshape(TOKENS, HEADS, HEAD_DIM)
    scaled = gain[None] * out_grad.astype(f32)
    width = HEADS * HEAD_DIM
    meansq = lax.optimization_barrier(jnp.sum(attn * attn, axis=(1, 2))) / width + EPSILON
    cross = lax.optimization_barrier(jnp.sum(scaled * attn, axis=(1, 2))) / width
    dattn = (lax.rsqrt(meansq)[:, None, None] * (scaled - attn * (cross / meansq)[:, None, None])).astype(jnp.bfloat16)

    def backward(state, block):
        qry, key_blk, val, dout, sg, bg, state_key = block
        mask, first, last, cut = block_layout(sg, bg)
        qf, kf, vf, df = (qry.astype(f32), key_blk.astype(f32), val.astype(f32), dout.astype(f32))
        skf = state_key.astype(f32)
        sgf = state.astype(jnp.bfloat16).astype(f32)
        scores = jnp.einsum('ihd,jhd->hij', qf, kf)
        probs = jnp.where(mask[None], scores, 0.0).astype(jnp.bfloat16).astype(f32)
        dprobs = jnp.where(mask[None], jnp.einsum('ihe,jhe->hij', df, vf), 0.0).astype(jnp.bfloat16).astype(f32)
        dq = jnp.einsum('hij,jhd->ihd', dprobs, kf) + jnp.where(first, jnp.einsum('ihe,hde->ihd', df, skf), 0.0)
        dk = jnp.einsum('hij,ihd->jhd', dprobs, qf) + jnp.where(last, jnp.einsum('jhe,hde->jhd', vf, sgf), 0.0)
        dv = jnp.einsum('hij,ihe->jhe', probs, df) + jnp.where(last, jnp.einsum('jhd,hde->jhe', kf, sgf), 0.0)
        head_part = jnp.einsum('ihd,ihe->hde', qf * first.astype(f32), df)
        grads = (dq.astype(jnp.bfloat16), dk.astype(jnp.bfloat16), dv.astype(jnp.bfloat16))
        return (head_part + (1.0 - cut) * state, grads)
    inputs = (blocks(queries), blocks(keys), blocks(values), blocks(dattn), blocks(seg), blocks(begins), key_states)
    unused, (dq_b, dk_b, dv_b) = lax.scan(backward, zero_state, inputs, reverse=True)
    shape = (TOKENS, HEADS, HEAD_DIM)
    return (dq_b.reshape(shape), dk_b.reshape(shape), dv_b.reshape(shape))
```

```python
import functools

import jax
import jax.numpy as jnp
from jax import lax
from jax.experimental import pallas as pl
from jax.experimental.pallas import tpu as pltpu
from jax.sharding import PartitionSpec as P

HEADS = 32
HEAD_DIM = 128
EPSILON = 1e-06
ZS, YS, XS = 8, 4, 4
CHIPS = ZS * YS
TOK = 256
LH = 8
HALF = 4
ROWS = HALF * HEAD_DIM
SL = ROWS // CHIPS
MESH = pl.DeviceIdType.MESH
f32 = jnp.float32
bf16 = jnp.bfloat16


def nt(a, b):
    return lax.dot_general(a, b, (((1,), (1,)), ((), ())), preferred_element_type=f32)


def nn(a, b):
    return lax.dot_general(a, b, (((1,), (0,)), ((), ())), preferred_element_type=f32)


def tn(a, b):
    return lax.dot_general(a, b, (((0,), (0,)), ((), ())), preferred_element_type=f32)


def kernel(
    starts, gain, q_in, k_in, v_in, g_in, oq, ok, ov,
    raw, tmp, qh, kh, vh, sc, mask, mask_t, first_m, last_m, probs_t, inner, attn, dat, dps, dqp, dkp, dvp,
    tme, toth, tsib, pbuf, fr, pb, sbuf, snd, stb, state, xb,
    in_sem, pair_s, pair_r, fwd_s, fwd_r, ret_s, ret_r, back_s, back_r, x_s, x_r,
):
    b = lax.axis_index("ctx")
    x = lax.axis_index("head")
    c = lax.rem(b, 2)
    m = b // 2
    oc = 1 - c
    sib = {"ctx": m * 2 + oc, "head": x}

    def chip(t):
        return {"ctx": t * 2 + c, "head": x}

    loads = [
        pltpu.make_async_copy(src, raw.at[n], in_sem.at[n])
        for n, src in enumerate((k_in, v_in, q_in, g_in))
    ]
    for load in loads:
        load.start()

    bar = pltpu.get_barrier_semaphore()
    pl.semaphore_signal(bar, inc=1, device_id=sib, device_id_type=MESH)
    for d in range(1, XS):
        pl.semaphore_signal(
            bar, inc=1, device_id={"ctx": b, "head": lax.rem(x + d, XS)}, device_id_type=MESH
        )

    @pl.loop(1, CHIPS)
    def _(d):
        pl.semaphore_signal(bar, inc=1, device_id=chip(lax.rem(m + d, CHIPS)), device_id_type=MESH)

    st = [starts[n] for n in range(4)]

    def seg_of(pos):
        total = (pos >= st[0]).astype(jnp.int32)
        for n in range(1, 4):
            total = total + (pos >= st[n]).astype(jnp.int32)
        return total

    def keep(lo, size):
        hit = (st[0] >= lo) & (st[0] < lo + size)
        for n in range(1, 4):
            hit = hit | ((st[n] >= lo) & (st[n] < lo + size))
        return jnp.where(hit, 0.0, 1.0).astype(f32)

    base = b * TOK
    row_c = lax.broadcasted_iota(jnp.int32, (TOK, HEAD_DIM), 0) + base
    seg_c = seg_of(row_c)
    begins0 = (base == st[0]) | (base == st[1]) | (base == st[2]) | (base == st[3])
    seg0 = jnp.where(begins0, -1, seg_of(base))
    first_m[...] = (seg_c == seg0).astype(f32)
    last_m[...] = (seg_c == seg_of(base + TOK - 1)).astype(f32)

    def relayout(n, out):
        tmp[...] = raw[n].astype(f32).reshape(TOK * LH, HEAD_DIM)
        for h in range(LH):
            out[h] = tmp[pl.ds(h, TOK, stride=LH), :].astype(out.dtype)

    loads[0].wait()
    relayout(0, kh)
    loads[1].wait()
    relayout(1, vh)

    def tail_of(h):
        return tn((kh[h].astype(f32) * last_m[...]).astype(bf16), vh[h])

    def pair_copy(src, dst, ss, rs):
        return pltpu.make_async_remote_copy(
            src_ref=src, dst_ref=dst, send_sem=ss, recv_sem=rs, device_id=sib, device_id_type=MESH
        )

    for r in range(HALF):
        toth[0, r * HEAD_DIM : (r + 1) * HEAD_DIM] = tail_of(oc * HALF + r)
    pl.semaphore_wait(bar, CHIPS + XS - 1)

    def scan(s, make_mine, w_me, w_sib, middle, reverse):
        first_pair = pair_copy(toth.at[s], tsib.at[s], pair_s.at[s], pair_r.at[s])
        first_pair.start()
        make_mine()
        first_pair.wait()
        pbuf[s] = tme[s] * w_me + tsib[s] * w_sib
        fr[s, pl.ds(m, 1)] = pbuf[s, pl.ds(pl.multiple_of(m * SL, SL), SL)][None]

        @pl.loop(1, CHIPS)
        def _(d):
            t = lax.rem(m + d, CHIPS)
            pltpu.make_async_remote_copy(
                src_ref=pbuf.at[s, pl.ds(pl.multiple_of(t * SL, SL), SL)],
                dst_ref=fr.at[s, m],
                send_sem=fwd_s.at[s],
                recv_sem=fwd_r.at[s],
                device_id=chip(t),
                device_id_type=MESH,
            ).start()

        middle()
        others = pl.ds(0, CHIPS - 1)
        whole = pltpu.make_async_copy(fr.at[s, others], fr.at[s, others], fwd_r.at[s])
        whole.wait()

        def step(n, carry):
            t = CHIPS - 1 - n if reverse else n
            pb[s, pl.ds(t, 1)] = carry[None]
            return fr[s, t] + keep(t * 2 * TOK, 2 * TOK) * carry

        lax.fori_loop(0, CHIPS, step, jnp.zeros((SL, HEAD_DIM), f32), unroll=True)
        sbuf[s, pl.ds(m, 1)] = pb[s, pl.ds(m, 1)]

        @pl.loop(1, CHIPS)
        def _(d):
            t = lax.rem(m + d, CHIPS)
            pltpu.make_async_remote_copy(
                src_ref=pb.at[s, t],
                dst_ref=sbuf.at[s, m],
                send_sem=ret_s.at[s],
                recv_sem=ret_r.at[s],
                device_id=chip(t),
                device_id_type=MESH,
            ).start()

        whole = pltpu.make_async_copy(sbuf.at[s, others], sbuf.at[s, others], ret_r.at[s])
        whole.wait()
        edge = 1 if reverse else 0
        whole_state = sbuf[s].reshape(ROWS, HEAD_DIM)
        is_edge = c == edge
        inner_part = jnp.where(is_edge, tme[s], tsib[s])
        away = inner_part + keep((2 * m + edge) * TOK, TOK) * whole_state
        snd[s] = jnp.where(is_edge, away, whole_state)
        back = pair_copy(snd.at[s], stb.at[s], back_s.at[s], back_r.at[s])
        back.start()
        mine = jnp.where(is_edge, whole_state, away).astype(bf16)
        state[s, pl.ds(c * HALF, HALF)] = mine.reshape(HALF, HEAD_DIM, HEAD_DIM)
        back.wait()
        state[s, pl.ds(oc * HALF, HALF)] = stb[s].astype(bf16).reshape(HALF, HEAD_DIM, HEAD_DIM)
        sent = pltpu.make_async_copy(fr.at[s, others], fr.at[s, others], fwd_s.at[s])
        sent.wait()
        sent = pltpu.make_async_copy(sbuf.at[s, others], sbuf.at[s, others], ret_s.at[s])
        sent.wait()

    def my_tails():
        for r in range(HALF):
            tme[0, r * HEAD_DIM : (r + 1) * HEAD_DIM] = tail_of(c * HALF + r)

    def middle_fwd():
        loads[2].wait()
        relayout(2, qh)
        loads[3].wait()
        relayout(3, sc)
        ri = lax.broadcasted_iota(jnp.int32, (TOK, TOK), 0)
        ci = lax.broadcasted_iota(jnp.int32, (TOK, TOK), 1)
        same = seg_of(ri + base) == seg_of(ci + base)
        mask[...] = ((ri >= ci) & same).astype(f32)
        mask_t[...] = ((ri <= ci) & same).astype(f32)

        @pl.loop(0, LH)
        def _(h):
            sc[h] = sc[h] * gain[pl.ds(h, 1), :]
            p = (nt(qh[h], kh[h]) * mask[...]).astype(bf16)
            probs_t[h] = (nt(kh[h], qh[h]) * mask_t[...]).astype(bf16)
            inner[h] = nn(p, vh[h])

    keep_even = keep(2 * m * TOK, TOK)
    keep_odd = keep((2 * m + 1) * TOK, TOK)
    one = jnp.ones((), f32)
    scan(
        0,
        my_tails,
        jnp.where(c == 0, keep_odd, one),
        jnp.where(c == 0, one, keep_odd),
        middle_fwd,
        False,
    )

    def attn_step(h, sums):
        a = inner[h] + first_m[...] * nn(qh[h], state[0, h])
        attn[h] = a
        return sums[0] + a * a, sums[1] + a * sc[h]

    zero = jnp.zeros((TOK, HEAD_DIM), f32)
    sq, cr = lax.fori_loop(0, LH, attn_step, (zero, zero))
    sq_row = jnp.sum(sq.T, axis=0, keepdims=True)
    cr_row = jnp.sum(cr.T, axis=0, keepdims=True)
    which = lax.broadcasted_iota(jnp.int32, (8, TOK), 0)
    xb[pl.ds(x, 1)] = jnp.where(which == 0, sq_row, cr_row)[None]
    for d in range(1, XS):
        pltpu.make_async_remote_copy(
            src_ref=xb.at[x],
            dst_ref=xb.at[x],
            send_sem=x_s,
            recv_sem=x_r,
            device_id={"ctx": b, "head": lax.rem(x + d, XS)},
            device_id_type=MESH,
        ).start()
    pltpu.make_async_copy(xb.at[pl.ds(0, XS - 1)], xb.at[pl.ds(0, XS - 1)], x_r).wait()
    tot = xb[0] + xb[1] + xb[2] + xb[3]
    width = HEADS * HEAD_DIM
    meansq = tot[0:1] / width + EPSILON
    cross = tot[1:2] / width
    rr = jnp.broadcast_to(lax.rsqrt(meansq), (HEAD_DIM, TOK)).T
    co = jnp.broadcast_to(cross / meansq, (HEAD_DIM, TOK)).T

    @pl.loop(0, LH)
    def _(h):
        dat[h] = (rr * (sc[h] - attn[h] * co)).astype(bf16)

    def head_of(h):
        return tn((qh[h].astype(f32) * first_m[...]).astype(bf16), dat[h])

    for r in range(HALF):
        toth[1, r * HEAD_DIM : (r + 1) * HEAD_DIM] = head_of(oc * HALF + r)

    def my_heads():
        for r in range(HALF):
            tme[1, r * HEAD_DIM : (r + 1) * HEAD_DIM] = head_of(c * HALF + r)

    def middle_bwd():
        for h in range(LH):
            dp = (nt(dat[h], vh[h]) * mask[...]).astype(bf16)
            dpt = (nt(vh[h], dat[h]) * mask_t[...]).astype(bf16)
            dq = nn(dp, kh[h]) + first_m[...] * nt(dat[h], state[0, h])
            tmp[pl.ds(h, TOK, stride=LH), :] = dq
            dkp[h] = nn(dpt, qh[h])
            dvp[h] = nn(probs_t[h], dat[h])
        oq[...] = tmp[...].reshape(TOK, LH, HEAD_DIM).astype(bf16)

    scan(
        1,
        my_heads,
        jnp.where(c == 1, keep_even, one),
        jnp.where(c == 1, one, keep_even),
        middle_bwd,
        True,
    )
    for h in range(LH):
        tmp[pl.ds(h, TOK, stride=LH), :] = dkp[h] + last_m[...] * nt(vh[h], state[1, h])
    ok[...] = tmp[...].reshape(TOK, LH, HEAD_DIM).astype(bf16)
    for h in range(LH):
        tmp[pl.ds(h, TOK, stride=LH), :] = dvp[h] + last_m[...] * nn(kh[h], state[1, h])
    ov[...] = tmp[...].reshape(TOK, LH, HEAD_DIM).astype(bf16)
    pltpu.make_async_copy(xb.at[pl.ds(0, XS - 1)], xb.at[pl.ds(0, XS - 1)], x_s).wait()


def local(queries, keys, values, out_grad, gain, starts):
    vm = pl.BlockSpec(memory_space=pltpu.VMEM)
    hb = pl.BlockSpec(memory_space=pl.ANY)
    out = jax.ShapeDtypeStruct((TOK, LH, HEAD_DIM), bf16)
    V = pltpu.VMEM
    D = pltpu.SemaphoreType.DMA
    return pl.pallas_call(
        kernel,
        out_shape=(out, out, out),
        in_specs=[pl.BlockSpec(memory_space=pltpu.SMEM), vm, hb, hb, hb, hb],
        out_specs=(vm, vm, vm),
        scratch_shapes=[
            V((4, TOK, LH, HEAD_DIM), bf16),
            V((TOK * LH, HEAD_DIM), f32),
            V((LH, TOK, HEAD_DIM), bf16),
            V((LH, TOK, HEAD_DIM), bf16),
            V((LH, TOK, HEAD_DIM), bf16),
            V((LH, TOK, HEAD_DIM), f32),
            V((TOK, TOK), f32),
            V((TOK, TOK), f32),
            V((TOK, HEAD_DIM), f32),
            V((TOK, HEAD_DIM), f32),
            V((LH, TOK, TOK), bf16),
            V((LH, TOK, HEAD_DIM), f32),
            V((LH, TOK, HEAD_DIM), f32),
            V((LH, TOK, HEAD_DIM), bf16),
            V((8, HEAD_DIM), f32),
            V((8, HEAD_DIM), f32),
            V((LH, TOK, HEAD_DIM), f32),
            V((LH, TOK, HEAD_DIM), f32),
            V((2, ROWS, HEAD_DIM), f32),
            V((2, ROWS, HEAD_DIM), f32),
            V((2, ROWS, HEAD_DIM), f32),
            V((2, ROWS, HEAD_DIM), f32),
            V((2, CHIPS, SL, HEAD_DIM), f32),
            V((2, CHIPS, SL, HEAD_DIM), f32),
            V((2, CHIPS, SL, HEAD_DIM), f32),
            V((2, ROWS, HEAD_DIM), f32),
            V((2, ROWS, HEAD_DIM), f32),
            V((2, LH, HEAD_DIM, HEAD_DIM), bf16),
            V((XS, 8, TOK), f32),
            D((4,)),
            D((2,)),
            D((2,)),
            D((2,)),
            D((2,)),
            D((2,)),
            D((2,)),
            D((2,)),
            D((2,)),
            D,
            D,
        ],
        compiler_params=pltpu.CompilerParams(
            collective_id=0, has_side_effects=True, vmem_limit_bytes=48 * 2**20
        ),
        cost_estimate=pl.CostEstimate(
            flops=1_400_000_000, bytes_accessed=4_000_000, transcendentals=2048
        ),
        name="fused",
    )(starts, gain, queries, keys, values, out_grad)


def solution(mesh):
    spec = P("ctx", "head", None)
    return jax.shard_map(
        local,
        mesh=mesh,
        in_specs=(spec, spec, spec, spec, P("head", None), P()),
        out_specs=(spec, spec, spec),
        check_vma=False,
    )
```

```python
import jax
import jax.numpy as jnp
from jax import lax
from jax.experimental import pallas as pl
from jax.experimental.pallas import tpu as pltpu
from jax.sharding import PartitionSpec as P

HEADS = 32
HEAD_DIM = 128
EPSILON = 1e-06
ZS, YS, XS = 8, 4, 4
CHIPS = ZS * YS
TOK = 256
LH = 8
HALF = 4
GROUPS = 2
GH = HALF // GROUPS
ROWS = GH * HEAD_DIM
SL = ROWS // CHIPS
CHUNK = 64
PIECES = 4
MESH = pl.DeviceIdType.MESH
f32 = jnp.float32
bf16 = jnp.bfloat16


def nt(a, b):
    return lax.dot_general(a, b, (((1,), (1,)), ((), ())), preferred_element_type=f32)


def nn(a, b):
    return lax.dot_general(a, b, (((1,), (0,)), ((), ())), preferred_element_type=f32)


def tn(a, b):
    return lax.dot_general(a, b, (((0,), (0,)), ((), ())), preferred_element_type=f32)


def kernel(
    starts_in, gain_in, q_in, k_in, v_in, g_in, oq, tk, tv,
    starts, gain, raw, tmp, qh, kh, vh, sc, mask, mask_t, first_m, last_m, qft, probs_t, inner, attn, dat, dkp, dvp,
    sqp, crp, rr, co, keeps, tme, toth, tsib, pbuf, fr, pb, sbuf, snd, stb, state, xb,
    in_sem, pair_s, pair_r, fwd_s, fwd_r, ret_s, ret_r, back_s, back_r, x_s, x_r,
):
    b = lax.axis_index("ctx")
    x = lax.axis_index("head")
    c = lax.rem(b, 2)
    m = b // 2
    mz = m // YS
    my = lax.rem(m, YS)
    oc = 1 - c
    sib = {"ctx": m * 2 + oc, "head": x}

    def chip(t):
        return {"ctx": t * 2 + c, "head": x}

    loads = [
        pltpu.make_async_copy(src, dst, in_sem.at[n])
        for n, (src, dst) in enumerate(
            (
                (starts_in, starts),
                (k_in, raw.at[0]),
                (v_in, raw.at[1]),
                (q_in, raw.at[2]),
                (g_in, raw.at[3]),
                (gain_in, gain),
            )
        )
    ]
    for load in loads:
        load.start()

    bar = pltpu.get_barrier_semaphore()
    pl.semaphore_signal(bar, inc=1, device_id=sib, device_id_type=MESH)
    for d in range(1, XS):
        pl.semaphore_signal(
            bar, inc=1, device_id={"ctx": b, "head": lax.rem(x + d, XS)}, device_id_type=MESH
        )

    def far_first(n):
        i = n // YS
        j = lax.rem(n, YS)
        dz = ZS // 2 + (1 - 2 * lax.rem(i, 2)) * ((i + 1) // 2)
        dy = YS // 2 + (1 - 2 * lax.rem(j, 2)) * ((j + 1) // 2)
        return lax.rem(mz + dz, ZS) * YS + lax.rem(my + dy, YS)

    @pl.loop(0, CHIPS - 1)
    def _(n):
        pl.semaphore_signal(bar, inc=1, device_id=chip(far_first(n)), device_id_type=MESH)

    loads[0].wait()
    st = [starts[n] for n in range(4)]

    def seg_of(pos):
        total = (pos >= st[0]).astype(jnp.int32)
        for n in range(1, 4):
            total = total + (pos >= st[n]).astype(jnp.int32)
        return total

    def keep(lo, size):
        hit = (st[0] >= lo) & (st[0] < lo + size)
        for n in range(1, 4):
            hit = hit | ((st[n] >= lo) & (st[n] < lo + size))
        return jnp.where(hit, 0.0, 1.0).astype(f32)

    base = b * TOK
    row_c = lax.broadcasted_iota(jnp.int32, (TOK, HEAD_DIM), 0) + base
    seg_c = seg_of(row_c)
    begins0 = (base == st[0]) | (base == st[1]) | (base == st[2]) | (base == st[3])
    seg0 = jnp.where(begins0, -1, seg_of(base))
    first_m[...] = (seg_c == seg0).astype(f32)
    last_m[...] = (seg_c == seg_of(base + TOK - 1)).astype(f32)

    def relayout(n, out, tmp):
        tmp[...] = raw[n].astype(f32).reshape(TOK * LH, HEAD_DIM)
        for h in range(LH):
            out[h] = tmp[pl.ds(h, TOK, stride=LH), :].astype(out.dtype)

    loads[1].wait()
    relayout(0, kh, tk)
    loads[2].wait()
    relayout(1, vh, tv)

    def tail_of(h):
        return tn((kh[h].astype(f32) * last_m[...]).astype(bf16), vh[h])

    def head_of(h):
        return nn(qft[h], dat[h])

    def pair_copy(src, dst, ss, rs):
        return pltpu.make_async_remote_copy(
            src_ref=src, dst_ref=dst, send_sem=ss, recv_sem=rs, device_id=sib, device_id_type=MESH
        )

    def to_all(src_of, dst, ss, rs):
        @pl.loop(0, CHIPS - 1)
        def _(n):
            t = far_first(n)
            pltpu.make_async_remote_copy(
                src_ref=src_of(t),
                dst_ref=dst.at[m],
                send_sem=ss,
                recv_sem=rs,
                device_id=chip(t),
                device_id_type=MESH,
            ).start()

    def bytes_of_others(buf, sem):
        part = buf.at[pl.ds(0, CHIPS - 1)]
        pltpu.make_async_copy(part, part, sem).wait()

    def sums(s, g, part_of):
        for r in range(GH):
            toth[s * GROUPS + g, r * HEAD_DIM : (r + 1) * HEAD_DIM] = part_of(oc * HALF + g * GH + r)

    def scan(s, part_of, w_me, w_sib, middle, late, use, reverse):
        at = [s * GROUPS + g for g in range(GROUPS)]
        firsts = [
            pair_copy(toth.at[i], tsib.at[i], pair_s.at[i], pair_r.at[i]) for i in at
        ]
        for g, i in enumerate(at):
            sums(s, g, part_of)
            if s == 0 and g == 0:
                pl.semaphore_wait(bar, CHIPS + XS - 1)
            firsts[g].start()
        for g, i in enumerate(at):
            for r in range(GH):
                tme[i, r * HEAD_DIM : (r + 1) * HEAD_DIM] = part_of(c * HALF + g * GH + r)
            firsts[g].wait_recv()
            pbuf[i] = (tme[i] * w_me + tsib[i] * w_sib).reshape(CHIPS, SL, HEAD_DIM)
            to_all(lambda t, i=i: pbuf.at[i, t], fr.at[i], fwd_s.at[i], fwd_r.at[i])
            fr[i, pl.ds(m, 1)] = pbuf[i, pl.ds(m, 1)]
        middle()
        for i in at:
            bytes_of_others(fr.at[i], fwd_r.at[i])
            carry = jnp.zeros((SL, HEAD_DIM), f32)
            for n in range(CHIPS):
                t = CHIPS - 1 - n if reverse else n
                pb[i, t] = carry
                carry = fr[i, t] + keeps[t] * carry
            to_all(lambda t, i=i: pb.at[i, t], sbuf.at[i], ret_s.at[i], ret_r.at[i])
            sbuf[i, pl.ds(m, 1)] = pb[i, pl.ds(m, 1)]
        late()
        edge = 1 if reverse else 0
        is_edge = c == edge
        edge_keep = keep((2 * m + edge) * TOK, TOK)
        backs = [pair_copy(snd.at[i], stb.at[i], back_s.at[i], back_r.at[i]) for i in at]
        for g, i in enumerate(at):
            bytes_of_others(sbuf.at[i], ret_r.at[i])
            whole = sbuf[i].reshape(ROWS, HEAD_DIM)
            away = jnp.where(is_edge, tme[i], tsib[i]) + edge_keep * whole
            snd[i] = jnp.where(is_edge, away, whole)
            backs[g].start()
            mine = jnp.where(is_edge, whole, away).astype(bf16)
            state[s, pl.ds(c * HALF + g * GH, GH)] = mine.reshape(GH, HEAD_DIM, HEAD_DIM)
        for g, i in enumerate(at):
            backs[g].wait_recv()
            theirs = stb[i].astype(bf16)
            state[s, pl.ds(oc * HALF + g * GH, GH)] = theirs.reshape(GH, HEAD_DIM, HEAD_DIM)
            use(g, [k * HALF + g * GH + r for k in range(2) for r in range(GH)])

    def near_fwd(h):
        p = (nt(qh[h], kh[h]) * mask[...]).astype(bf16)
        probs_t[h] = (nt(kh[h], qh[h]) * mask_t[...]).astype(bf16)
        inner[h] = nn(p, vh[h])
        qft[h] = (qh[h].astype(f32) * first_m[...]).T.astype(bf16)

    def middle_fwd():
        chip_row = lax.broadcasted_iota(jnp.int32, (CHIPS, SL, HEAD_DIM), 0)
        keeps[...] = keep(chip_row * (2 * TOK), 2 * TOK)
        loads[3].wait()
        relayout(2, qh, tk)
        ri = lax.broadcasted_iota(jnp.int32, (TOK, TOK), 0)
        ci = lax.broadcasted_iota(jnp.int32, (TOK, TOK), 1)
        same = seg_of(ri + base) == seg_of(ci + base)
        mask[...] = ((ri >= ci) & same).astype(f32)
        mask_t[...] = ((ri <= ci) & same).astype(f32)
        for h in range(HALF):
            near_fwd(h)

    def late_fwd():
        for h in range(HALF, LH):
            near_fwd(h)
        loads[4].wait()
        loads[5].wait()
        relayout(3, sc, tv)
        for h in range(LH):
            sc[h] = sc[h] * gain[h : h + 1, :]

    def use_fwd(g, hs):
        for lo in range(0, TOK, CHUNK):
            rows = pl.ds(lo, CHUNK)
            sq = jnp.zeros((CHUNK, HEAD_DIM), f32)
            cr = jnp.zeros((CHUNK, HEAD_DIM), f32)
            for h in hs:
                a = inner[h, rows] + first_m[rows] * nn(qh[h, rows], state[0, h])
                attn[h, rows] = a
                sq = sq + a * a
                cr = cr + a * sc[h, rows]
            sqp[g, rows] = sq
            crp[g, rows] = cr

    keep_even = keep(2 * m * TOK, TOK)
    keep_odd = keep((2 * m + 1) * TOK, TOK)
    one = jnp.ones((), f32)
    scan(
        0,
        tail_of,
        jnp.where(c == 0, keep_odd, one),
        jnp.where(c == 0, one, keep_odd),
        middle_fwd,
        late_fwd,
        use_fwd,
        False,
    )

    sq_row = jnp.sum((sqp[0] + sqp[1]).T, axis=0, keepdims=True)
    cr_row = jnp.sum((crp[0] + crp[1]).T, axis=0, keepdims=True)
    which = lax.broadcasted_iota(jnp.int32, (8, TOK), 0)
    xb[pl.ds(x, 1)] = jnp.where(which == 0, sq_row, cr_row)[None]
    for d in (2, 1, 3):
        pltpu.make_async_remote_copy(
            src_ref=xb.at[x],
            dst_ref=xb.at[x],
            send_sem=x_s,
            recv_sem=x_r,
            device_id={"ctx": b, "head": lax.rem(x + d, XS)},
            device_id_type=MESH,
        ).start()
    pltpu.make_async_copy(xb.at[pl.ds(0, XS - 1)], xb.at[pl.ds(0, XS - 1)], x_r).wait()
    tot = xb[0] + xb[1] + xb[2] + xb[3]
    width = HEADS * HEAD_DIM
    meansq = tot[0:1] / width + EPSILON
    cross = tot[1:2] / width
    rr[...] = jnp.broadcast_to(lax.rsqrt(meansq), (HEAD_DIM, TOK)).T
    co[...] = jnp.broadcast_to(cross / meansq, (HEAD_DIM, TOK)).T

    def dattn_head(h):
        dat[h] = (rr[...] * (sc[h] - attn[h] * co[...])).astype(bf16)
        return head_of(h)

    def near_bwd(h):
        dp = (nt(dat[h], vh[h]) * mask[...]).astype(bf16)
        dpt = (nt(vh[h], dat[h]) * mask_t[...]).astype(bf16)
        dq = nn(dp, kh[h]) + first_m[...] * nt(dat[h], state[0, h])
        tmp[pl.ds(h, TOK, stride=LH), :] = dq
        dkp[h] = nn(dpt, qh[h])
        dvp[h] = nn(probs_t[h], dat[h])

    def middle_bwd():
        for h in range(HALF):
            near_bwd(h)

    def late_bwd():
        for h in range(HALF, LH):
            near_bwd(h)
        oq[...] = tmp[...].reshape(TOK, LH, HEAD_DIM).astype(bf16)

    def use_bwd(g, hs):
        for h in hs:
            at = pl.ds(h, TOK, stride=LH)
            tk[at, :] = dkp[h] + last_m[...] * nt(vh[h], state[1, h])
            tv[at, :] = dvp[h] + last_m[...] * nn(kh[h], state[1, h])

    scan(
        1,
        dattn_head,
        jnp.where(c == 1, keep_even, one),
        jnp.where(c == 1, one, keep_even),
        middle_bwd,
        late_bwd,
        use_bwd,
        True,
    )
    pltpu.make_async_copy(xb.at[pl.ds(0, XS - 1)], xb.at[pl.ds(0, XS - 1)], x_s).wait()
    for i in range(2 * GROUPS):
        pair_copy(toth.at[i], tsib.at[i], pair_s.at[i], pair_r.at[i]).wait_send()
        pair_copy(snd.at[i], stb.at[i], back_s.at[i], back_r.at[i]).wait_send()
        bytes_of_others(fr.at[i], fwd_s.at[i])
        bytes_of_others(sbuf.at[i], ret_s.at[i])


def finish(oq, tk, tv, out_q, out_k, out_v, buf, sem):
    pltpu.make_async_copy(oq, out_q, sem.at[0]).start()
    for n, (src, dst) in enumerate(((tk, out_k), (tv, out_v))):
        for p in range(PIECES):
            rows = pl.ds(p * TOK // PIECES, TOK // PIECES)
            flat = pl.ds(p * TOK * LH // PIECES, TOK * LH // PIECES)
            buf[n, rows] = src[flat, :].reshape(TOK // PIECES, LH, HEAD_DIM).astype(bf16)
            pltpu.make_async_copy(buf.at[n, rows], dst.at[rows], sem.at[1 + n * PIECES + p]).start()
    pltpu.make_async_copy(oq, out_q, sem.at[0]).wait()
    for n, dst in enumerate((out_k, out_v)):
        for p in range(PIECES):
            rows = pl.ds(p * TOK // PIECES, TOK // PIECES)
            pltpu.make_async_copy(buf.at[n, rows], dst.at[rows], sem.at[1 + n * PIECES + p]).wait()


def local(queries, keys, values, out_grad, gain, starts):
    vm = pl.BlockSpec(memory_space=pltpu.VMEM)
    hb = pl.BlockSpec(memory_space=pltpu.HBM)
    args = [
        pltpu.with_memory_space_constraint(a, pltpu.HBM)
        for a in (starts, gain, queries, keys, values, out_grad)
    ]
    flat = jax.ShapeDtypeStruct((TOK * LH, HEAD_DIM), f32)
    out = jax.ShapeDtypeStruct((TOK, LH, HEAD_DIM), bf16)
    V = pltpu.VMEM
    D = pltpu.SemaphoreType.DMA
    N = 2 * GROUPS
    heads16 = V((LH, TOK, HEAD_DIM), bf16)
    heads32 = V((LH, TOK, HEAD_DIM), f32)
    cols = V((TOK, HEAD_DIM), f32)
    part = V((N, ROWS, HEAD_DIM), f32)
    slices = V((N, CHIPS, SL, HEAD_DIM), f32)
    parts = pl.pallas_call(
        kernel,
        out_shape=(out, flat, flat),
        in_specs=[hb] * 6,
        out_specs=(vm, vm, vm),
        scratch_shapes=[
            pltpu.SMEM((4,), jnp.int32),
            V((LH, HEAD_DIM), f32),
            V((4, TOK, LH, HEAD_DIM), bf16),
            V((TOK * LH, HEAD_DIM), f32),
            heads16,
            heads16,
            heads16,
            heads32,
            V((TOK, TOK), f32),
            V((TOK, TOK), f32),
            cols,
            cols,
            V((LH, HEAD_DIM, TOK), bf16),
            V((LH, TOK, TOK), bf16),
            heads32,
            heads32,
            heads16,
            heads32,
            heads32,
            V((2, TOK, HEAD_DIM), f32),
            V((2, TOK, HEAD_DIM), f32),
            cols,
            cols,
            V((CHIPS, SL, HEAD_DIM), f32),
            part,
            part,
            part,
            slices,
            slices,
            slices,
            slices,
            part,
            part,
            V((2, LH, HEAD_DIM, HEAD_DIM), bf16),
            V((XS, 8, TOK), f32),
            D((6,)),
            D((N,)),
            D((N,)),
            D((N,)),
            D((N,)),
            D((N,)),
            D((N,)),
            D((N,)),
            D((N,)),
            D,
            D,
        ],
        compiler_params=pltpu.CompilerParams(
            collective_id=0, has_side_effects=True, vmem_limit_bytes=32 * 2**20
        ),
        cost_estimate=pl.CostEstimate(
            flops=1_400_000_000, bytes_accessed=4_000_000, transcendentals=2048
        ),
        name="fused",
    )(*args)
    return pl.pallas_call(
        finish,
        out_shape=(out, out, out),
        in_specs=[vm] * 3,
        out_specs=(hb, hb, hb),
        scratch_shapes=[V((2, TOK, LH, HEAD_DIM), bf16), D((1 + 2 * PIECES,))],
        compiler_params=pltpu.CompilerParams(vmem_limit_bytes=4 * 2**20),
        name="finish",
    )(*parts)


def solution(mesh):
    spec = P("ctx", "head", None)
    return jax.shard_map(
        local,
        mesh=mesh,
        in_specs=(spec, spec, spec, spec, P("head", None), P()),
        out_specs=(spec, spec, spec),
        check_vma=False,
    )
```

```python
import jax
import jax.numpy as jnp
from jax import lax
from jax.experimental import pallas as pl
from jax.experimental.pallas import tpu as pltpu
from jax.sharding import PartitionSpec as P

HEADS = 32
HEAD_DIM = 128
EPSILON = 1e-06
ZS, YS, XS = 8, 4, 4
CHIPS = ZS * YS
TOK = 256
LH = 8
HALF = 4
GROUPS = 2
GH = HALF // GROUPS
ROWS = GH * HEAD_DIM
SL = ROWS // CHIPS
CHUNK = 64
PIECES = 4
FAR = sorted(
    ((dz, dy) for dz in range(ZS) for dy in range(YS) if dz or dy),
    key=lambda o: -(min(o[0], ZS - o[0]) + min(o[1], YS - o[1])),
)
MESH = pl.DeviceIdType.MESH
f32 = jnp.float32
bf16 = jnp.bfloat16


def nt(a, b):
    return lax.dot_general(a, b, (((1,), (1,)), ((), ())), preferred_element_type=f32)


def nn(a, b):
    return lax.dot_general(a, b, (((1,), (0,)), ((), ())), preferred_element_type=f32)


def tn(a, b):
    return lax.dot_general(a, b, (((0,), (0,)), ((), ())), preferred_element_type=f32)


def kernel(
    starts_in, gain_in, q_in, k_in, v_in, g_in, oq, tk, tv,
    starts, gain, raw, tmp, qh, kh, vh, sc, mask, mask_t, first_m, last_m, probs_t, dat, dkp, dvp,
    xin, xat, xsc, yin, ysc, yq, rq, yd, rd, xq, qft, st,
    sqp, crp, rr, co, keeps, tme, toth, tsib, hodd, pbuf, fr, pb, sbuf, snd, stb, xb, tot,
    in_sem, pair_s, pair_r, fwd_s, fwd_r, ret_s, ret_r, back_s, back_r, ex_s, ex_r, yd_s, yd_r, x_s, x_r,
):
    b = lax.axis_index("ctx")
    x = lax.axis_index("head")
    c = lax.rem(b, 2)
    m = b // 2
    mz = m // YS
    my = lax.rem(m, YS)
    oc = 1 - c
    sib = {"ctx": m * 2 + oc, "head": x}

    def chip(t):
        return {"ctx": t * 2 + c, "head": x}

    loads = [
        pltpu.make_async_copy(src, dst, in_sem.at[n])
        for n, (src, dst) in enumerate(
            (
                (starts_in, starts),
                (k_in, raw.at[0]),
                (v_in, raw.at[1]),
                (q_in, raw.at[2]),
                (g_in, raw.at[3]),
                (gain_in, gain),
            )
        )
    ]

    def others(n):
        return lax.rem(mz + FAR[n][0], ZS) * YS + lax.rem(my + FAR[n][1], YS)

    peers = [
        {"ctx": m * 2 + lax.rem(c + e, 2), "head": lax.rem(x + d, XS)}
        for d in (2, 1, 3, 0)
        for e in (1, 0)
        if (d, e) != (0, 0)
    ]
    bar = pltpu.get_barrier_semaphore()
    for n in range(CHIPS - 1):
        pl.semaphore_signal(bar, inc=1, device_id=chip(others(n)), device_id_type=MESH)
    for peer in peers:
        pl.semaphore_signal(bar, inc=1, device_id=peer, device_id_type=MESH)
    for load in loads:
        load.start()

    loads[0].wait()
    sv = [starts[n] for n in range(4)]

    def seg_of(pos):
        total = (pos >= sv[0]).astype(jnp.int32)
        for n in range(1, 4):
            total = total + (pos >= sv[n]).astype(jnp.int32)
        return total

    def keep(lo, size):
        hit = (sv[0] >= lo) & (sv[0] < lo + size)
        for n in range(1, 4):
            hit = hit | ((sv[n] >= lo) & (sv[n] < lo + size))
        return jnp.where(hit, 0.0, 1.0).astype(f32)

    base = b * TOK
    row_c = lax.broadcasted_iota(jnp.int32, (TOK, HEAD_DIM), 0) + base
    seg_c = seg_of(row_c)
    begins0 = (base == sv[0]) | (base == sv[1]) | (base == sv[2]) | (base == sv[3])
    seg0 = jnp.where(begins0, -1, seg_of(base))
    first_m[...] = (seg_c == seg0).astype(f32)
    last_m[...] = (seg_c == seg_of(base + TOK - 1)).astype(f32)
    keep_even = keep(2 * m * TOK, TOK)
    keep_odd = keep((2 * m + 1) * TOK, TOK)

    def relayout(n, out, tmp):
        tmp[...] = raw[n].astype(f32).reshape(TOK * LH, HEAD_DIM)
        for h in range(LH):
            out[h] = tmp[pl.ds(h, TOK, stride=LH), :].astype(out.dtype)

    def pair_copy(src, dst, ss, rs):
        return pltpu.make_async_remote_copy(
            src_ref=src, dst_ref=dst, send_sem=ss, recv_sem=rs, device_id=sib, device_id_type=MESH
        )

    def to_all(src, dst, ss, rs):
        for n in range(CHIPS - 1):
            t = others(n)
            pltpu.make_async_remote_copy(
                src_ref=src.at[t],
                dst_ref=dst.at[m],
                send_sem=ss,
                recv_sem=rs,
                device_id=chip(t),
                device_id_type=MESH,
            ).start()

    def bytes_of(buf, count, sem):
        part = buf.at[pl.ds(0, count)]
        pltpu.make_async_copy(part, part, sem).wait()

    def rows_of(r):
        return pl.ds(r * HEAD_DIM, HEAD_DIM)

    def forward(i, p):
        pbuf[i] = p.reshape(CHIPS, SL, HEAD_DIM)
        to_all(pbuf.at[i], fr.at[i], fwd_s.at[i], fwd_r.at[i])
        fr[i, pl.ds(m, 1)] = pbuf[i, pl.ds(m, 1)]

    def turn(i, reverse):
        bytes_of(fr.at[i], CHIPS - 1, fwd_r.at[i])
        carry = jnp.zeros((SL, HEAD_DIM), f32)
        for n in range(CHIPS):
            t = CHIPS - 1 - n if reverse else n
            pb[i, t] = carry
            carry = fr[i, t] + keeps[t] * carry
        to_all(pb.at[i], sbuf.at[i], ret_s.at[i], ret_r.at[i])
        sbuf[i, pl.ds(m, 1)] = pb[i, pl.ds(m, 1)]

    def split(i, edge, part, weight):
        bytes_of(sbuf.at[i], CHIPS - 1, ret_r.at[i])
        whole = sbuf[i].reshape(ROWS, HEAD_DIM)
        away = part + weight * whole
        is_edge = c == edge
        snd[i] = jnp.where(is_edge, away, whole)
        pair_copy(snd.at[i], stb.at[i], back_s.at[i], back_r.at[i]).start()
        return jnp.where(is_edge, whole, away)

    loads[1].wait()
    relayout(0, kh, tk)
    loads[2].wait()
    relayout(1, vh, tv)

    def tail_of(h):
        return tn((kh[h].astype(f32) * last_m[...]).astype(bf16), vh[h])

    for g in range(GROUPS):
        for r in range(GH):
            toth[g, rows_of(r)] = tail_of(oc * HALF + g * GH + r)
    for g in range(GROUPS):
        for r in range(GH):
            tme[g, rows_of(r)] = tail_of(c * HALF + g * GH + r)
    pl.semaphore_wait(bar, CHIPS - 1 + len(peers))
    one = jnp.ones((), f32)
    w_me = jnp.where(c == 0, keep_odd, one)
    w_sib = jnp.where(c == 0, one, keep_odd)
    firsts = [pair_copy(toth.at[g], tsib.at[g], pair_s.at[g], pair_r.at[g]) for g in range(GROUPS)]
    for g in range(GROUPS):
        firsts[g].start()
    for g in range(GROUPS):
        firsts[g].wait_recv()
        forward(g, tme[g] * w_me + tsib[g] * w_sib)

    chip_row = lax.broadcasted_iota(jnp.int32, (CHIPS, SL, HEAD_DIM), 0)
    keeps[...] = keep(chip_row * (2 * TOK), 2 * TOK)
    loads[3].wait()
    relayout(2, qh, tk)
    ri = lax.broadcasted_iota(jnp.int32, (TOK, TOK), 0)
    ci = lax.broadcasted_iota(jnp.int32, (TOK, TOK), 1)
    same = seg_of(ri + base) == seg_of(ci + base)
    mask[...] = ((ri >= ci) & same).astype(f32)
    mask_t[...] = ((ri <= ci) & same).astype(f32)

    def near_fwd(h):
        p = (nt(qh[h], kh[h]) * mask[...]).astype(bf16)
        probs_t[h] = (nt(kh[h], qh[h]) * mask_t[...]).astype(bf16)
        return nn(p, vh[h])

    swaps = [
        pair_copy(src, dst, ex_s.at[n], ex_r.at[n])
        for n, (src, dst) in enumerate(((yin, xin.at[1]), (yq, rq), (ysc, xsc.at[1])))
    ]
    for r in range(HALF):
        h = oc * HALF + r
        yq[r] = qh[h].astype(f32) * first_m[...]
        yin[r] = near_fwd(h)
    swaps[0].start()
    swaps[1].start()
    turn(0, False)
    turn(1, False)
    loads[4].wait()
    loads[5].wait()
    relayout(3, sc, tv)
    for r in range(HALF):
        ysc[r] = sc[oc * HALF + r] * gain[pl.ds(oc * HALF + r, 1), :]
    swaps[2].start()
    for r in range(HALF):
        h = c * HALF + r
        xsc[0, r] = sc[h] * gain[pl.ds(h, 1), :]
        masked = qh[h].astype(f32) * first_m[...]
        xq[0, r] = masked.astype(bf16)
        qft[0, r] = masked.T.astype(bf16)
        xin[0, r] = near_fwd(h)
    swaps[1].wait_recv()
    for r in range(HALF):
        xq[1, r] = rq[r].astype(bf16)
        qft[1, r] = rq[r].T.astype(bf16)
    swaps[0].wait_recv()
    swaps[2].wait_recv()

    for g in range(GROUPS):
        own = split(g, 0, jnp.where(c == 0, tme[g], tsib[g]), keep_even)
        st[0, g * GH : (g + 1) * GH] = own.astype(bf16).reshape(GH, HEAD_DIM, HEAD_DIM)
        st[1, g * GH : (g + 1) * GH] = snd[g].astype(bf16).reshape(GH, HEAD_DIM, HEAD_DIM)
        for j in range(2):
            for lo in range(0, TOK, CHUNK):
                rows = pl.ds(lo, CHUNK)
                sq = jnp.zeros((CHUNK, HEAD_DIM), f32)
                cr = jnp.zeros((CHUNK, HEAD_DIM), f32)
                for r in range(g * GH, (g + 1) * GH):
                    a = xin[j, r, rows] + nn(xq[j, r, rows], st[j, r])
                    xat[j, r, rows] = a
                    sq = sq + a * a
                    cr = cr + a * xsc[j, r, rows]
                sqp[g, j, rows] = sq
                crp[g, j, rows] = cr

    which = lax.broadcasted_iota(jnp.int32, (8, HEAD_DIM), 0)
    tile = jnp.zeros((8, HEAD_DIM), f32)
    for j, core in enumerate((c, oc)):
        for n, part in enumerate((sqp, crp)):
            line = jnp.sum((part[0, j] + part[1, j]).T, axis=0, keepdims=True)
            for k in range(2):
                half = line[:, k * HEAD_DIM : (k + 1) * HEAD_DIM]
                tile = jnp.where(which == n * 4 + core * 2 + k, half, tile)
    slot = x * 2 + c
    xb[pl.ds(slot, 1)] = tile[None]
    for peer in peers:
        pltpu.make_async_remote_copy(
            src_ref=xb.at[slot],
            dst_ref=xb.at[slot],
            send_sem=x_s,
            recv_sem=x_r,
            device_id=peer,
            device_id_type=MESH,
        ).start()
    bytes_of(xb, len(peers), x_r)
    total = xb[0]
    for n in range(1, 2 * XS):
        total = total + xb[n]
    width = HEADS * HEAD_DIM
    meansq = total[0:4] / width + EPSILON
    cross = total[4:8] / width
    tot[0:4] = lax.rsqrt(meansq)
    tot[4:8] = cross / meansq
    for j, core in enumerate((c, oc)):
        for k in range(2):
            rows = pl.ds(k * HEAD_DIM, HEAD_DIM)
            for n, out in enumerate((rr, co)):
                line = tot[pl.ds(n * 4 + core * 2 + k, 1), :]
                out[j, rows] = jnp.broadcast_to(line, (HEAD_DIM, HEAD_DIM)).T

    gives = [pair_copy(yd.at[g], rd.at[g], yd_s.at[g], yd_r.at[g]) for g in range(GROUPS)]
    for g in range(GROUPS):
        parts = []
        for r in range(GH):
            at = g * GH + r
            pair = []
            for j in range(2):
                d = rr[j] * (xsc[j, at] - xat[j, at] * co[j])
                d = d.astype(bf16)
                if j == 0:
                    dat[c * HALF + at] = d
                else:
                    yd[g, r] = d.astype(f32)
                pair.append(nn(qft[j, at], d))
            even = jnp.where(c == 0, pair[0], pair[1])
            odd = jnp.where(c == 0, pair[1], pair[0])
            hodd[g, rows_of(r)] = odd
            parts.append(even + keep_even * odd)
        forward(GROUPS + g, jnp.concatenate(parts, axis=0))
        gives[g].start()

    def near_bwd(h, state):
        dp = (nt(dat[h], vh[h]) * mask[...]).astype(bf16)
        dpt = (nt(vh[h], dat[h]) * mask_t[...]).astype(bf16)
        dq = nn(dp, kh[h]) + first_m[...] * nt(dat[h], state)
        tmp[pl.ds(h, TOK, stride=LH), :] = dq
        dkp[h] = nn(dpt, qh[h])
        dvp[h] = nn(probs_t[h], dat[h])

    for r in range(HALF):
        near_bwd(c * HALF + r, st[0, r])
    for g in range(GROUPS):
        turn(GROUPS + g, True)
    for g in range(GROUPS):
        pair_copy(snd.at[g], stb.at[g], back_s.at[g], back_r.at[g]).wait_recv()
        gives[g].wait_recv()
        for r in range(GH):
            h = oc * HALF + g * GH + r
            dat[h] = rd[g, r].astype(bf16)
            near_bwd(h, stb[g, rows_of(r)].astype(bf16))
    oq[...] = tmp[...].reshape(TOK, LH, HEAD_DIM).astype(bf16)

    def last_of(h, state):
        at = pl.ds(h, TOK, stride=LH)
        tk[at, :] = dkp[h] + last_m[...] * nt(vh[h], state)
        tv[at, :] = dvp[h] + last_m[...] * nn(kh[h], state)

    for g in range(GROUPS):
        own = split(GROUPS + g, 1, hodd[g], keep_odd).astype(bf16)
        for r in range(GH):
            last_of(c * HALF + g * GH + r, own[r * HEAD_DIM : (r + 1) * HEAD_DIM])
    for g in range(GROUPS):
        i = GROUPS + g
        pair_copy(snd.at[i], stb.at[i], back_s.at[i], back_r.at[i]).wait_recv()
        for r in range(GH):
            last_of(oc * HALF + g * GH + r, stb[i, rows_of(r)].astype(bf16))

    bytes_of(xb, len(peers), x_s)
    for swap in swaps:
        swap.wait_send()
    for g in range(GROUPS):
        firsts[g].wait_send()
        gives[g].wait_send()
    for i in range(2 * GROUPS):
        pair_copy(snd.at[i], stb.at[i], back_s.at[i], back_r.at[i]).wait_send()
        bytes_of(fr.at[i], CHIPS - 1, fwd_s.at[i])
        bytes_of(sbuf.at[i], CHIPS - 1, ret_s.at[i])


def finish(oq, tk, tv, out_q, out_k, out_v, buf, sem):
    pltpu.make_async_copy(oq, out_q, sem.at[0]).start()
    for n, (src, dst) in enumerate(((tk, out_k), (tv, out_v))):
        for p in range(PIECES):
            rows = pl.ds(p * TOK // PIECES, TOK // PIECES)
            flat = pl.ds(p * TOK * LH // PIECES, TOK * LH // PIECES)
            buf[n, rows] = src[flat, :].reshape(TOK // PIECES, LH, HEAD_DIM).astype(bf16)
            pltpu.make_async_copy(buf.at[n, rows], dst.at[rows], sem.at[1 + n * PIECES + p]).start()
    pltpu.make_async_copy(oq, out_q, sem.at[0]).wait()
    for n, dst in enumerate((out_k, out_v)):
        for p in range(PIECES):
            rows = pl.ds(p * TOK // PIECES, TOK // PIECES)
            pltpu.make_async_copy(buf.at[n, rows], dst.at[rows], sem.at[1 + n * PIECES + p]).wait()


def local(queries, keys, values, out_grad, gain, starts):
    vm = pl.BlockSpec(memory_space=pltpu.VMEM)
    hb = pl.BlockSpec(memory_space=pltpu.HBM)
    args = [
        pltpu.with_memory_space_constraint(a, pltpu.HBM)
        for a in (starts, gain, queries, keys, values, out_grad)
    ]
    flat = jax.ShapeDtypeStruct((TOK * LH, HEAD_DIM), f32)
    out = jax.ShapeDtypeStruct((TOK, LH, HEAD_DIM), bf16)
    V = pltpu.VMEM
    D = pltpu.SemaphoreType.DMA
    N = 2 * GROUPS
    heads16 = V((LH, TOK, HEAD_DIM), bf16)
    heads32 = V((LH, TOK, HEAD_DIM), f32)
    cols = V((TOK, HEAD_DIM), f32)
    half32 = V((HALF, TOK, HEAD_DIM), f32)
    both32 = V((2, HALF, TOK, HEAD_DIM), f32)
    part = V((GROUPS, ROWS, HEAD_DIM), f32)
    parts2 = V((N, ROWS, HEAD_DIM), f32)
    slices = V((N, CHIPS, SL, HEAD_DIM), f32)
    parts = pl.pallas_call(
        kernel,
        out_shape=(out, flat, flat),
        in_specs=[hb] * 6,
        out_specs=(vm, vm, vm),
        scratch_shapes=[
            pltpu.SMEM((4,), jnp.int32),
            V((LH, HEAD_DIM), f32),
            V((4, TOK, LH, HEAD_DIM), bf16),
            V((TOK * LH, HEAD_DIM), f32),
            heads16,
            heads16,
            heads16,
            heads32,
            V((TOK, TOK), f32),
            V((TOK, TOK), f32),
            cols,
            cols,
            V((LH, TOK, TOK), bf16),
            heads16,
            heads32,
            heads32,
            both32,
            both32,
            both32,
            half32,
            half32,
            half32,
            half32,
            V((GROUPS, GH, TOK, HEAD_DIM), f32),
            V((GROUPS, GH, TOK, HEAD_DIM), f32),
            V((2, HALF, TOK, HEAD_DIM), bf16),
            V((2, HALF, HEAD_DIM, TOK), bf16),
            V((2, HALF, HEAD_DIM, HEAD_DIM), bf16),
            V((GROUPS, 2, TOK, HEAD_DIM), f32),
            V((GROUPS, 2, TOK, HEAD_DIM), f32),
            V((2, TOK, HEAD_DIM), f32),
            V((2, TOK, HEAD_DIM), f32),
            V((CHIPS, SL, HEAD_DIM), f32),
            part,
            part,
            part,
            part,
            slices,
            slices,
            slices,
            slices,
            parts2,
            parts2,
            V((2 * XS, 8, HEAD_DIM), f32),
            V((8, HEAD_DIM), f32),
            D((6,)),
            D((GROUPS,)),
            D((GROUPS,)),
            D((N,)),
            D((N,)),
            D((N,)),
            D((N,)),
            D((N,)),
            D((N,)),
            D((3,)),
            D((3,)),
            D((GROUPS,)),
            D((GROUPS,)),
            D,
            D,
        ],
        compiler_params=pltpu.CompilerParams(
            collective_id=0, has_side_effects=True, vmem_limit_bytes=32 * 2**20
        ),
        cost_estimate=pl.CostEstimate(
            flops=1_400_000_000, bytes_accessed=4_000_000, transcendentals=2048
        ),
        name="fused",
    )(*args)
    return pl.pallas_call(
        finish,
        out_shape=(out, out, out),
        in_specs=[vm] * 3,
        out_specs=(hb, hb, hb),
        scratch_shapes=[V((2, TOK, LH, HEAD_DIM), bf16), D((1 + 2 * PIECES,))],
        compiler_params=pltpu.CompilerParams(vmem_limit_bytes=4 * 2**20),
        name="finish",
    )(*parts)


def solution(mesh):
    spec = P("ctx", "head", None)
    return jax.shard_map(
        local,
        mesh=mesh,
        in_specs=(spec, spec, spec, spec, P("head", None), P()),
        out_specs=(spec, spec, spec),
        check_vma=False,
    )
```

```python
import jax
import jax.numpy as jnp
from jax import lax
from jax.experimental import pallas as pl
from jax.experimental.pallas import tpu as pltpu
from jax.sharding import PartitionSpec as P

HEADS = 32
HEAD_DIM = 128
EPSILON = 1e-06
ZS, YS, XS = 8, 4, 4
CHIPS = ZS * YS
TOK = 256
LH = 8
HALF = 4
GROUPS = 2
GH = HALF // GROUPS
ROWS = GH * HEAD_DIM
SL = ROWS // CHIPS
CHUNK = 64
EARLY = 1
PIECES = 4
FAR = sorted(
    ((dz, dy) for dz in range(ZS) for dy in range(YS) if dz or dy),
    key=lambda o: -(min(o[0], ZS - o[0]) + min(o[1], YS - o[1])),
)
MESH = pl.DeviceIdType.MESH
f32 = jnp.float32
bf16 = jnp.bfloat16


def nt(a, b):
    return lax.dot_general(a, b, (((1,), (1,)), ((), ())), preferred_element_type=f32)


def nn(a, b):
    return lax.dot_general(a, b, (((1,), (0,)), ((), ())), preferred_element_type=f32)


def tn(a, b):
    return lax.dot_general(a, b, (((0,), (0,)), ((), ())), preferred_element_type=f32)


def kernel(
    starts_in, gain_in, q_in, k_in, v_in, g_in, oq, tk, tv,
    starts, gain, raw, tmp, qh, kh, vh, sc, mask, mask_t, first_m, last_m, probs_t, dat, dkp, dvp,
    xin, xat, xsc, yin, ysc, yq, rq, yd, rd, xq, qft, st,
    sqp, crp, rr, co, keeps, tme, toth, tsib, hodd, pbuf, fr, pb, sbuf, direct, snd, stb, xb, tot,
    in_sem, pair_s, pair_r, fwd_s, fwd_r, ret_s, ret_r, dir_s, dir_r, back_s, back_r, ex_s, ex_r, yd_s, yd_r, x_s, x_r,
):
    b = lax.axis_index("ctx")
    x = lax.axis_index("head")
    c = lax.rem(b, 2)
    m = b // 2
    mz = m // YS
    my = lax.rem(m, YS)
    oc = 1 - c
    sib = {"ctx": m * 2 + oc, "head": x}

    def chip(t):
        return {"ctx": t * 2 + c, "head": x}

    loads = [
        pltpu.make_async_copy(src, dst, in_sem.at[n])
        for n, (src, dst) in enumerate(
            (
                (starts_in, starts),
                (k_in, raw.at[0]),
                (v_in, raw.at[1]),
                (q_in, raw.at[2]),
                (g_in, raw.at[3]),
                (gain_in, gain),
            )
        )
    ]

    def others(n):
        return lax.rem(mz + FAR[n][0], ZS) * YS + lax.rem(my + FAR[n][1], YS)

    peers = [
        {"ctx": m * 2 + lax.rem(c + e, 2), "head": lax.rem(x + d, XS)}
        for d in (2, 1, 3, 0)
        for e in (1, 0)
        if (d, e) != (0, 0)
    ]
    bar = pltpu.get_barrier_semaphore()
    for n in range(CHIPS - 1):
        pl.semaphore_signal(bar, inc=1, device_id=chip(others(n)), device_id_type=MESH)
    for peer in peers:
        pl.semaphore_signal(bar, inc=1, device_id=peer, device_id_type=MESH)
    for load in loads:
        load.start()

    loads[0].wait()
    sv = [starts[n] for n in range(4)]

    def seg_of(pos):
        total = (pos >= sv[0]).astype(jnp.int32)
        for n in range(1, 4):
            total = total + (pos >= sv[n]).astype(jnp.int32)
        return total

    def keep(lo, size):
        hit = (sv[0] >= lo) & (sv[0] < lo + size)
        for n in range(1, 4):
            hit = hit | ((sv[n] >= lo) & (sv[n] < lo + size))
        return jnp.where(hit, 0.0, 1.0).astype(f32)

    base = b * TOK
    row_c = lax.broadcasted_iota(jnp.int32, (TOK, HEAD_DIM), 0) + base
    seg_c = seg_of(row_c)
    begins0 = (base == sv[0]) | (base == sv[1]) | (base == sv[2]) | (base == sv[3])
    seg0 = jnp.where(begins0, -1, seg_of(base))
    first_m[...] = (seg_c == seg0).astype(f32)
    last_m[...] = (seg_c == seg_of(base + TOK - 1)).astype(f32)
    keep_even = keep(2 * m * TOK, TOK)
    keep_odd = keep((2 * m + 1) * TOK, TOK)

    def relayout(n, out, tmp):
        tmp[...] = raw[n].astype(f32).reshape(TOK * LH, HEAD_DIM)
        for h in range(LH):
            out[h] = tmp[pl.ds(h, TOK, stride=LH), :].astype(out.dtype)

    def pair_copy(src, dst, ss, rs):
        return pltpu.make_async_remote_copy(
            src_ref=src, dst_ref=dst, send_sem=ss, recv_sem=rs, device_id=sib, device_id_type=MESH
        )

    def slice_copy(src, dst, ss, rs, t, core):
        return pltpu.make_async_remote_copy(
            src_ref=src.at[t],
            dst_ref=dst.at[m],
            send_sem=ss,
            recv_sem=rs,
            device_id={"ctx": t * 2 + core, "head": x},
            device_id_type=MESH,
        )

    def to_all(src, dst, ss, rs, lead=False):
        for n in range(CHIPS - 1):
            t = others(n)
            if lead and n == 0:
                t = t * (1 - (m + CHIPS - 1) // CHIPS)
            elif lead:
                t = t + (1 - (t + CHIPS - 1) // CHIPS) * others(0)
            slice_copy(src, dst, ss, rs, t, c).start()

    def bytes_of(buf, count, sem):
        part = buf.at[pl.ds(0, count)]
        pltpu.make_async_copy(part, part, sem).wait()

    def rows_of(r):
        return pl.ds(r * HEAD_DIM, HEAD_DIM)

    def forward(i, p):
        pbuf[i] = p.reshape(CHIPS, SL, HEAD_DIM)
        to_all(pbuf.at[i], fr.at[i], fwd_s.at[i], fwd_r.at[i])
        fr[i, pl.ds(m, 1)] = pbuf[i, pl.ds(m, 1)]

    def turn(i, reverse):
        bytes_of(fr.at[i], CHIPS - 1, fwd_r.at[i])
        carry = jnp.zeros((SL, HEAD_DIM), f32)
        for n in range(CHIPS):
            t = CHIPS - 1 - n if reverse else n
            pb[i, t] = carry
            carry = fr[i, t] + keeps[t] * carry
        if reverse:
            g = i - GROUPS

            @pl.when(c == 0)
            def _():
                for t in range(EARLY):
                    slice_copy(pb.at[i], direct.at[g], dir_s.at[g], dir_r.at[g], t, 1).start()

        to_all(pb.at[i], sbuf.at[i], ret_s.at[i], ret_r.at[i])
        sbuf[i, pl.ds(m, 1)] = pb[i, pl.ds(m, 1)]

    def split(i, edge, part, weight):
        bytes_of(sbuf.at[i], CHIPS - 1, ret_r.at[i])
        whole = sbuf[i].reshape(ROWS, HEAD_DIM)
        away = part + weight * whole
        is_edge = c == edge
        snd[i] = jnp.where(is_edge, away, whole)

        @pl.when(jnp.logical_or(edge == 0, jnp.logical_or(c == 1, m >= EARLY)))
        def _():
            pair_copy(snd.at[i], stb.at[i], back_s.at[i], back_r.at[i]).start()

        return jnp.where(is_edge, whole, away)

    loads[1].wait()
    relayout(0, kh, tk)
    loads[2].wait()
    relayout(1, vh, tv)

    def tail_of(h):
        return tn((kh[h].astype(f32) * last_m[...]).astype(bf16), vh[h])

    for g in range(GROUPS):
        for r in range(GH):
            toth[g, rows_of(r)] = tail_of(oc * HALF + g * GH + r)
    for g in range(GROUPS):
        for r in range(GH):
            tme[g, rows_of(r)] = tail_of(c * HALF + g * GH + r)
    pl.semaphore_wait(bar, CHIPS - 1 + len(peers))
    one = jnp.ones((), f32)
    w_me = jnp.where(c == 0, keep_odd, one)
    w_sib = jnp.where(c == 0, one, keep_odd)
    firsts = [pair_copy(toth.at[g], tsib.at[g], pair_s.at[g], pair_r.at[g]) for g in range(GROUPS)]
    for g in range(GROUPS):
        firsts[g].start()
    for g in range(GROUPS):
        firsts[g].wait_recv()
        forward(g, tme[g] * w_me + tsib[g] * w_sib)

    chip_row = lax.broadcasted_iota(jnp.int32, (CHIPS, SL, HEAD_DIM), 0)
    keeps[...] = keep(chip_row * (2 * TOK), 2 * TOK)
    loads[3].wait()
    relayout(2, qh, tk)
    ri = lax.broadcasted_iota(jnp.int32, (TOK, TOK), 0)
    ci = lax.broadcasted_iota(jnp.int32, (TOK, TOK), 1)
    same = seg_of(ri + base) == seg_of(ci + base)
    mask[...] = ((ri >= ci) & same).astype(f32)
    mask_t[...] = ((ri <= ci) & same).astype(f32)

    def near_fwd(h):
        p = (nt(qh[h], kh[h]) * mask[...]).astype(bf16)
        probs_t[h] = (nt(kh[h], qh[h]) * mask_t[...]).astype(bf16)
        return nn(p, vh[h])

    swaps = [
        pair_copy(src, dst, ex_s.at[n], ex_r.at[n])
        for n, (src, dst) in enumerate(((yin, xin.at[1]), (yq, rq), (ysc, xsc.at[1])))
    ]
    for r in range(HALF):
        h = oc * HALF + r
        yq[r] = qh[h].astype(f32) * first_m[...]
        yin[r] = near_fwd(h)
    swaps[0].start()
    swaps[1].start()
    turn(0, False)
    turn(1, False)
    loads[4].wait()
    loads[5].wait()
    relayout(3, sc, tv)
    for r in range(HALF):
        ysc[r] = sc[oc * HALF + r] * gain[pl.ds(oc * HALF + r, 1), :]
    swaps[2].start()
    for r in range(HALF):
        h = c * HALF + r
        xsc[0, r] = sc[h] * gain[pl.ds(h, 1), :]
        masked = qh[h].astype(f32) * first_m[...]
        xq[0, r] = masked.astype(bf16)
        qft[0, r] = masked.T.astype(bf16)
        xin[0, r] = near_fwd(h)
    swaps[1].wait_recv()
    for r in range(HALF):
        xq[1, r] = rq[r].astype(bf16)
        qft[1, r] = rq[r].T.astype(bf16)
    swaps[0].wait_recv()
    swaps[2].wait_recv()

    for g in range(GROUPS):
        own = split(g, 0, jnp.where(c == 0, tme[g], tsib[g]), keep_even)
        st[0, g * GH : (g + 1) * GH] = own.astype(bf16).reshape(GH, HEAD_DIM, HEAD_DIM)
        st[1, g * GH : (g + 1) * GH] = snd[g].astype(bf16).reshape(GH, HEAD_DIM, HEAD_DIM)
        for j in range(2):
            for lo in range(0, TOK, CHUNK):
                rows = pl.ds(lo, CHUNK)
                sq = jnp.zeros((CHUNK, HEAD_DIM), f32)
                cr = jnp.zeros((CHUNK, HEAD_DIM), f32)
                for r in range(g * GH, (g + 1) * GH):
                    a = xin[j, r, rows] + nn(xq[j, r, rows], st[j, r])
                    xat[j, r, rows] = a
                    sq = sq + a * a
                    cr = cr + a * xsc[j, r, rows]
                sqp[g, j, rows] = sq
                crp[g, j, rows] = cr

    which = lax.broadcasted_iota(jnp.int32, (8, HEAD_DIM), 0)
    tile = jnp.zeros((8, HEAD_DIM), f32)
    for j, core in enumerate((c, oc)):
        for n, part in enumerate((sqp, crp)):
            line = jnp.sum((part[0, j] + part[1, j]).T, axis=0, keepdims=True)
            for k in range(2):
                half = line[:, k * HEAD_DIM : (k + 1) * HEAD_DIM]
                tile = jnp.where(which == n * 4 + core * 2 + k, half, tile)
    slot = x * 2 + c
    xb[pl.ds(slot, 1)] = tile[None]
    for peer in peers:
        pltpu.make_async_remote_copy(
            src_ref=xb.at[slot],
            dst_ref=xb.at[slot],
            send_sem=x_s,
            recv_sem=x_r,
            device_id=peer,
            device_id_type=MESH,
        ).start()
    bytes_of(xb, len(peers), x_r)
    total = xb[0]
    for n in range(1, 2 * XS):
        total = total + xb[n]
    width = HEADS * HEAD_DIM
    meansq = total[0:4] / width + EPSILON
    cross = total[4:8] / width
    tot[0:4] = lax.rsqrt(meansq)
    tot[4:8] = cross / meansq
    for j, core in enumerate((c, oc)):
        for k in range(2):
            rows = pl.ds(k * HEAD_DIM, HEAD_DIM)
            for n, out in enumerate((rr, co)):
                line = tot[pl.ds(n * 4 + core * 2 + k, 1), :]
                out[j, rows] = jnp.broadcast_to(line, (HEAD_DIM, HEAD_DIM)).T

    gives = [pair_copy(yd.at[g], rd.at[g], yd_s.at[g], yd_r.at[g]) for g in range(GROUPS)]
    for g in range(GROUPS):
        parts = []
        for r in range(GH):
            at = g * GH + r
            pair = []
            for j in range(2):
                d = rr[j] * (xsc[j, at] - xat[j, at] * co[j])
                d = d.astype(bf16)
                if j == 0:
                    dat[c * HALF + at] = d
                else:
                    yd[g, r] = d.astype(f32)
                pair.append(nn(qft[j, at], d))
            even = jnp.where(c == 0, pair[0], pair[1])
            odd = jnp.where(c == 0, pair[1], pair[0])
            hodd[g, rows_of(r)] = odd
            parts.append(even + keep_even * odd)
        forward(GROUPS + g, jnp.concatenate(parts, axis=0))
        gives[g].start()

    def near_bwd(h, state):
        dp = (nt(dat[h], vh[h]) * mask[...]).astype(bf16)
        dpt = (nt(vh[h], dat[h]) * mask_t[...]).astype(bf16)
        dq = nn(dp, kh[h]) + first_m[...] * nt(dat[h], state)
        tmp[pl.ds(h, TOK, stride=LH), :] = dq
        dkp[h] = nn(dpt, qh[h])
        dvp[h] = nn(probs_t[h], dat[h])

    for r in range(HALF):
        near_bwd(c * HALF + r, st[0, r])
    for g in range(GROUPS):
        turn(GROUPS + g, True)
    for g in range(GROUPS):
        pair_copy(snd.at[g], stb.at[g], back_s.at[g], back_r.at[g]).wait_recv()
        gives[g].wait_recv()
        for r in range(GH):
            h = oc * HALF + g * GH + r
            dat[h] = rd[g, r].astype(bf16)
            near_bwd(h, stb[g, rows_of(r)].astype(bf16))
    oq[...] = tmp[...].reshape(TOK, LH, HEAD_DIM).astype(bf16)

    def last_of(h, state):
        at = pl.ds(h, TOK, stride=LH)
        tk[at, :] = dkp[h] + last_m[...] * nt(vh[h], state)
        tv[at, :] = dvp[h] + last_m[...] * nn(kh[h], state)

    def own_last(g):
        own = split(GROUPS + g, 1, hodd[g], keep_odd).astype(bf16)
        for r in range(GH):
            last_of(c * HALF + g * GH + r, own[r * HEAD_DIM : (r + 1) * HEAD_DIM])

    def other_last(g):
        i = GROUPS + g

        @pl.when(jnp.logical_or(c == 0, m >= EARLY))
        def _():
            pair_copy(snd.at[i], stb.at[i], back_s.at[i], back_r.at[i]).wait_recv()

        @pl.when(jnp.logical_and(c == 1, m < EARLY))
        def _():
            bytes_of(direct.at[g], CHIPS, dir_r.at[g])
            stb[i] = direct[g].reshape(ROWS, HEAD_DIM)

        for r in range(GH):
            last_of(oc * HALF + g * GH + r, stb[i, rows_of(r)].astype(bf16))

    own_last(0)
    own_last(1)
    other_last(0)
    other_last(1)

    bytes_of(xb, len(peers), x_s)
    for swap in swaps:
        swap.wait_send()
    for g in range(GROUPS):
        firsts[g].wait_send()
        gives[g].wait_send()
    for g in range(GROUPS):
        pair_copy(snd.at[g], stb.at[g], back_s.at[g], back_r.at[g]).wait_send()

        @pl.when(c == 0)
        def _(g=g):
            bytes_of(direct.at[g], EARLY, dir_s.at[g])

        @pl.when(jnp.logical_or(c == 1, m >= EARLY))
        def _(i=GROUPS + g):
            pair_copy(snd.at[i], stb.at[i], back_s.at[i], back_r.at[i]).wait_send()

    for i in range(2 * GROUPS):
        bytes_of(fr.at[i], CHIPS - 1, fwd_s.at[i])
        bytes_of(sbuf.at[i], CHIPS - 1, ret_s.at[i])


def finish(oq, tk, tv, out_q, out_k, out_v, buf, sem):
    pltpu.make_async_copy(oq, out_q, sem.at[0]).start()
    for n, (src, dst) in enumerate(((tk, out_k), (tv, out_v))):
        for p in range(PIECES):
            rows = pl.ds(p * TOK // PIECES, TOK // PIECES)
            flat = pl.ds(p * TOK * LH // PIECES, TOK * LH // PIECES)
            buf[n, rows] = src[flat, :].reshape(TOK // PIECES, LH, HEAD_DIM).astype(bf16)
            pltpu.make_async_copy(buf.at[n, rows], dst.at[rows], sem.at[1 + n * PIECES + p]).start()
    pltpu.make_async_copy(oq, out_q, sem.at[0]).wait()
    for n, dst in enumerate((out_k, out_v)):
        for p in range(PIECES):
            rows = pl.ds(p * TOK // PIECES, TOK // PIECES)
            pltpu.make_async_copy(buf.at[n, rows], dst.at[rows], sem.at[1 + n * PIECES + p]).wait()


def local(queries, keys, values, out_grad, gain, starts):
    vm = pl.BlockSpec(memory_space=pltpu.VMEM)
    hb = pl.BlockSpec(memory_space=pltpu.HBM)
    args = [
        pltpu.with_memory_space_constraint(a, pltpu.HBM)
        for a in (starts, gain, queries, keys, values, out_grad)
    ]
    flat = jax.ShapeDtypeStruct((TOK * LH, HEAD_DIM), f32)
    out = jax.ShapeDtypeStruct((TOK, LH, HEAD_DIM), bf16)
    V = pltpu.VMEM
    D = pltpu.SemaphoreType.DMA
    N = 2 * GROUPS
    heads16 = V((LH, TOK, HEAD_DIM), bf16)
    heads32 = V((LH, TOK, HEAD_DIM), f32)
    cols = V((TOK, HEAD_DIM), f32)
    half32 = V((HALF, TOK, HEAD_DIM), f32)
    both32 = V((2, HALF, TOK, HEAD_DIM), f32)
    part = V((GROUPS, ROWS, HEAD_DIM), f32)
    parts2 = V((N, ROWS, HEAD_DIM), f32)
    slices = V((N, CHIPS, SL, HEAD_DIM), f32)
    parts = pl.pallas_call(
        kernel,
        out_shape=(out, flat, flat),
        in_specs=[hb] * 6,
        out_specs=(vm, vm, vm),
        scratch_shapes=[
            pltpu.SMEM((4,), jnp.int32),
            V((LH, HEAD_DIM), f32),
            V((4, TOK, LH, HEAD_DIM), bf16),
            V((TOK * LH, HEAD_DIM), f32),
            heads16,
            heads16,
            heads16,
            heads32,
            V((TOK, TOK), f32),
            V((TOK, TOK), f32),
            cols,
            cols,
            V((LH, TOK, TOK), bf16),
            heads16,
            heads32,
            heads32,
            both32,
            both32,
            both32,
            half32,
            half32,
            half32,
            half32,
            V((GROUPS, GH, TOK, HEAD_DIM), f32),
            V((GROUPS, GH, TOK, HEAD_DIM), f32),
            V((2, HALF, TOK, HEAD_DIM), bf16),
            V((2, HALF, HEAD_DIM, TOK), bf16),
            V((2, HALF, HEAD_DIM, HEAD_DIM), bf16),
            V((GROUPS, 2, TOK, HEAD_DIM), f32),
            V((GROUPS, 2, TOK, HEAD_DIM), f32),
            V((2, TOK, HEAD_DIM), f32),
            V((2, TOK, HEAD_DIM), f32),
            V((CHIPS, SL, HEAD_DIM), f32),
            part,
            part,
            part,
            part,
            slices,
            slices,
            slices,
            slices,
            V((GROUPS, CHIPS, SL, HEAD_DIM), f32),
            parts2,
            parts2,
            V((2 * XS, 8, HEAD_DIM), f32),
            V((8, HEAD_DIM), f32),
            D((6,)),
            D((GROUPS,)),
            D((GROUPS,)),
            D((N,)),
            D((N,)),
            D((N,)),
            D((N,)),
            D((GROUPS,)),
            D((GROUPS,)),
            D((N,)),
            D((N,)),
            D((3,)),
            D((3,)),
            D((GROUPS,)),
            D((GROUPS,)),
            D,
            D,
        ],
        compiler_params=pltpu.CompilerParams(
            collective_id=0, has_side_effects=True, vmem_limit_bytes=32 * 2**20
        ),
        cost_estimate=pl.CostEstimate(
            flops=1_400_000_000, bytes_accessed=4_000_000, transcendentals=2048
        ),
        name="fused",
    )(*args)
    return pl.pallas_call(
        finish,
        out_shape=(out, out, out),
        in_specs=[vm] * 3,
        out_specs=(hb, hb, hb),
        scratch_shapes=[V((2, TOK, LH, HEAD_DIM), bf16), D((1 + 2 * PIECES,))],
        compiler_params=pltpu.CompilerParams(vmem_limit_bytes=4 * 2**20),
        name="finish",
    )(*parts)


def solution(mesh):
    spec = P("ctx", "head", None)
    return jax.shard_map(
        local,
        mesh=mesh,
        in_specs=(spec, spec, spec, spec, P("head", None), P()),
        out_specs=(spec, spec, spec),
        check_vma=False,
    )
```

```python
import jax
import jax.numpy as jnp
from jax import lax
from jax.experimental import pallas as pl
from jax.experimental.pallas import tpu as pltpu
from jax.sharding import PartitionSpec as P

HEADS = 32
HEAD_DIM = 128
EPSILON = 1e-06
ZS, YS, XS = 8, 4, 4
CHIPS = ZS * YS
TOK = 256
LH = 8
HALF = 4
GROUPS = 2
GH = HALF // GROUPS
ROWS = GH * HEAD_DIM
SL = ROWS // CHIPS
CHUNK = 64
EARLY = 1
PIECES = 4
FAR = sorted(
    ((dz, dy) for dz in range(ZS) for dy in range(YS) if dz or dy),
    key=lambda o: -(min(o[0], ZS - o[0]) + min(o[1], YS - o[1])),
)
MESH = pl.DeviceIdType.MESH
f32 = jnp.float32
bf16 = jnp.bfloat16


def nt(a, b):
    return lax.dot_general(a, b, (((1,), (1,)), ((), ())), preferred_element_type=f32)


def nn(a, b):
    return lax.dot_general(a, b, (((1,), (0,)), ((), ())), preferred_element_type=f32)


def tn(a, b):
    return lax.dot_general(a, b, (((0,), (0,)), ((), ())), preferred_element_type=f32)


def kernel(
    starts_in, gain_in, q_in, k_in, v_in, g_in, oq, tk, tv,
    starts, gain, raw, tmp, qh, kh, vh, sc, mask, mask_t, first_m, last_m, probs_t, dat, dkp, dvp,
    xin, xat, xsc, yin, ysc, yq, rq, yd, rd, xq, qft, st,
    sqp, crp, rr, co, keeps, tme, toth, tsib, hodd, pbuf, fr, pb, sbuf, direct, snd, stb, xb, tot,
    in_sem, pair_s, pair_r, fwd_s, fwd_r, ret_s, ret_r, dir_s, dir_r, back_s, back_r, ex_s, ex_r, yd_s, yd_r, x_s, x_r, hello, go,
):
    b = lax.axis_index("ctx")
    x = lax.axis_index("head")
    c = lax.rem(b, 2)
    m = b // 2
    mz = m // YS
    my = lax.rem(m, YS)
    oc = 1 - c
    sib = {"ctx": m * 2 + oc, "head": x}

    def chip(t):
        return {"ctx": t * 2 + c, "head": x}

    loads = [
        pltpu.make_async_copy(src, dst, in_sem.at[n])
        for n, (src, dst) in enumerate(
            (
                (starts_in, starts),
                (k_in, raw.at[0]),
                (v_in, raw.at[1]),
                (q_in, raw.at[2]),
                (g_in, raw.at[3]),
                (gain_in, gain),
            )
        )
    ]

    def others(n):
        return lax.rem(mz + FAR[n][0], ZS) * YS + lax.rem(my + FAR[n][1], YS)

    peers = [
        {"ctx": m * 2 + lax.rem(c + e, 2), "head": lax.rem(x + d, XS)}
        for d in (2, 1, 3, 0)
        for e in (1, 0)
        if (d, e) != (0, 0)
    ]
    bar = pltpu.get_barrier_semaphore()

    @pl.when(c == 1)
    def _():
        pl.semaphore_signal(bar, inc=1, device_id=sib, device_id_type=MESH)

    for n in range(CHIPS - 1):
        far = {"ctx": others(n) * 2 + 1, "head": x}
        pl.semaphore_signal(bar, inc=1, device_id=far, device_id_type=MESH)
    for d in (2, 1, 3):
        side = {"ctx": m * 2 + 1, "head": lax.rem(x + d, XS)}
        pl.semaphore_signal(bar, inc=1, device_id=side, device_id_type=MESH)
    for load in loads:
        load.start()

    @pl.when(c == 0)
    def _():
        pl.semaphore_wait(bar, 1)
        pl.semaphore_signal(hello, inc=1, device_id=sib, device_id_type=MESH)

    loads[0].wait()
    sv = [starts[n] for n in range(4)]

    def seg_of(pos):
        total = (pos >= sv[0]).astype(jnp.int32)
        for n in range(1, 4):
            total = total + (pos >= sv[n]).astype(jnp.int32)
        return total

    def keep(lo, size):
        hit = (sv[0] >= lo) & (sv[0] < lo + size)
        for n in range(1, 4):
            hit = hit | ((sv[n] >= lo) & (sv[n] < lo + size))
        return jnp.where(hit, 0.0, 1.0).astype(f32)

    base = b * TOK
    row_c = lax.broadcasted_iota(jnp.int32, (TOK, HEAD_DIM), 0) + base
    seg_c = seg_of(row_c)
    begins0 = (base == sv[0]) | (base == sv[1]) | (base == sv[2]) | (base == sv[3])
    seg0 = jnp.where(begins0, -1, seg_of(base))
    first_m[...] = (seg_c == seg0).astype(f32)
    last_m[...] = (seg_c == seg_of(base + TOK - 1)).astype(f32)
    keep_even = keep(2 * m * TOK, TOK)
    keep_odd = keep((2 * m + 1) * TOK, TOK)

    def relayout(n, out, tmp):
        tmp[...] = raw[n].astype(f32).reshape(TOK * LH, HEAD_DIM)
        for h in range(LH):
            out[h] = tmp[pl.ds(h, TOK, stride=LH), :].astype(out.dtype)

    def pair_copy(src, dst, ss, rs):
        return pltpu.make_async_remote_copy(
            src_ref=src, dst_ref=dst, send_sem=ss, recv_sem=rs, device_id=sib, device_id_type=MESH
        )

    def slice_copy(src, dst, ss, rs, t, core):
        return pltpu.make_async_remote_copy(
            src_ref=src.at[t],
            dst_ref=dst.at[m],
            send_sem=ss,
            recv_sem=rs,
            device_id={"ctx": t * 2 + core, "head": x},
            device_id_type=MESH,
        )

    def to_all(src, dst, ss, rs, lead=False):
        for n in range(CHIPS - 1):
            t = others(n)
            if lead and n == 0:
                t = t * (1 - (m + CHIPS - 1) // CHIPS)
            elif lead:
                t = t + (1 - (t + CHIPS - 1) // CHIPS) * others(0)
            slice_copy(src, dst, ss, rs, t, c).start()

    def bytes_of(buf, count, sem):
        part = buf.at[pl.ds(0, count)]
        pltpu.make_async_copy(part, part, sem).wait()

    def rows_of(r):
        return pl.ds(r * HEAD_DIM, HEAD_DIM)

    def forward(i):
        to_all(pbuf.at[i], fr.at[i], fwd_s.at[i], fwd_r.at[i])
        fr[i, pl.ds(m, 1)] = pbuf[i, pl.ds(m, 1)]

    def turn(i, reverse):
        bytes_of(fr.at[i], CHIPS - 1, fwd_r.at[i])
        carry = jnp.zeros((SL, HEAD_DIM), f32)
        for n in range(CHIPS):
            t = CHIPS - 1 - n if reverse else n
            pb[i, t] = carry
            carry = fr[i, t] + keeps[t] * carry
        if reverse:
            g = i - GROUPS

            @pl.when(c == 0)
            def _():
                for t in range(EARLY):
                    slice_copy(pb.at[i], direct.at[g], dir_s.at[g], dir_r.at[g], t, 1).start()

        to_all(pb.at[i], sbuf.at[i], ret_s.at[i], ret_r.at[i])
        sbuf[i, pl.ds(m, 1)] = pb[i, pl.ds(m, 1)]

    def split(i, edge, part, weight):
        bytes_of(sbuf.at[i], CHIPS - 1, ret_r.at[i])
        whole = sbuf[i].reshape(ROWS, HEAD_DIM)
        away = part + weight * whole
        is_edge = c == edge
        snd[i] = jnp.where(is_edge, away, whole)

        @pl.when(jnp.logical_or(edge == 0, jnp.logical_or(c == 1, m >= EARLY)))
        def _():
            pair_copy(snd.at[i], stb.at[i], back_s.at[i], back_r.at[i]).start()

        return jnp.where(is_edge, whole, away)

    loads[1].wait()
    relayout(0, kh, tk)
    loads[2].wait()
    relayout(1, vh, tv)

    def tail_of(h):
        return tn((kh[h].astype(f32) * last_m[...]).astype(bf16), vh[h])

    firsts = [pair_copy(toth.at[g], tsib.at[g], pair_s.at[g], pair_r.at[g]) for g in range(GROUPS)]
    for g in range(GROUPS):
        for r in range(GH):
            toth[g, rows_of(r)] = tail_of(oc * HALF + g * GH + r)
        if g == 0:

            @pl.when(c == 1)
            def _():
                pl.semaphore_wait(hello, 1)

        firsts[g].start()
    for g in range(GROUPS):
        for r in range(GH):
            tme[g, rows_of(r)] = tail_of(c * HALF + g * GH + r)
    one = jnp.ones((), f32)
    w_me = jnp.where(c == 0, keep_odd, one)
    w_sib = jnp.where(c == 0, one, keep_odd)
    for g in range(GROUPS):
        firsts[g].wait_recv()
        pbuf[g] = (tme[g] * w_me + tsib[g] * w_sib).reshape(CHIPS, SL, HEAD_DIM)

    @pl.when(c == 1)
    def _():
        pl.semaphore_wait(bar, 2 * (CHIPS - 1) + 2 * (XS - 1))
        pl.semaphore_signal(go, inc=1, device_id=sib, device_id_type=MESH)

    @pl.when(c == 0)
    def _():
        pl.semaphore_wait(go, 1)

    for g in range(GROUPS):
        forward(g)

    chip_row = lax.broadcasted_iota(jnp.int32, (CHIPS, SL, HEAD_DIM), 0)
    keeps[...] = keep(chip_row * (2 * TOK), 2 * TOK)
    loads[3].wait()
    relayout(2, qh, tk)
    ri = lax.broadcasted_iota(jnp.int32, (TOK, TOK), 0)
    ci = lax.broadcasted_iota(jnp.int32, (TOK, TOK), 1)
    same = seg_of(ri + base) == seg_of(ci + base)
    mask[...] = ((ri >= ci) & same).astype(f32)
    mask_t[...] = ((ri <= ci) & same).astype(f32)

    def near_fwd(h):
        p = (nt(qh[h], kh[h]) * mask[...]).astype(bf16)
        probs_t[h] = (nt(kh[h], qh[h]) * mask_t[...]).astype(bf16)
        return nn(p, vh[h])

    swaps = [
        pair_copy(src, dst, ex_s.at[n], ex_r.at[n])
        for n, (src, dst) in enumerate(((yin, xin.at[1]), (yq, rq), (ysc, xsc.at[1])))
    ]
    for r in range(HALF):
        h = oc * HALF + r
        yq[r] = qh[h].astype(f32) * first_m[...]
        yin[r] = near_fwd(h)
    swaps[0].start()
    swaps[1].start()
    turn(0, False)
    turn(1, False)
    loads[4].wait()
    loads[5].wait()
    relayout(3, sc, tv)
    for r in range(HALF):
        ysc[r] = sc[oc * HALF + r] * gain[pl.ds(oc * HALF + r, 1), :]
    swaps[2].start()
    for r in range(HALF):
        h = c * HALF + r
        xsc[0, r] = sc[h] * gain[pl.ds(h, 1), :]
        masked = qh[h].astype(f32) * first_m[...]
        xq[0, r] = masked.astype(bf16)
        qft[0, r] = masked.T.astype(bf16)
        xin[0, r] = near_fwd(h)
    swaps[1].wait_recv()
    for r in range(HALF):
        xq[1, r] = rq[r].astype(bf16)
        qft[1, r] = rq[r].T.astype(bf16)
    swaps[0].wait_recv()
    swaps[2].wait_recv()

    for g in range(GROUPS):
        own = split(g, 0, jnp.where(c == 0, tme[g], tsib[g]), keep_even)
        st[0, g * GH : (g + 1) * GH] = own.astype(bf16).reshape(GH, HEAD_DIM, HEAD_DIM)
        st[1, g * GH : (g + 1) * GH] = snd[g].astype(bf16).reshape(GH, HEAD_DIM, HEAD_DIM)
        for j in range(2):
            for lo in range(0, TOK, CHUNK):
                rows = pl.ds(lo, CHUNK)
                sq = jnp.zeros((CHUNK, HEAD_DIM), f32)
                cr = jnp.zeros((CHUNK, HEAD_DIM), f32)
                for r in range(g * GH, (g + 1) * GH):
                    a = xin[j, r, rows] + nn(xq[j, r, rows], st[j, r])
                    xat[j, r, rows] = a
                    sq = sq + a * a
                    cr = cr + a * xsc[j, r, rows]
                sqp[g, j, rows] = sq
                crp[g, j, rows] = cr

    which = lax.broadcasted_iota(jnp.int32, (8, HEAD_DIM), 0)
    tile = jnp.zeros((8, HEAD_DIM), f32)
    for j, core in enumerate((c, oc)):
        for n, part in enumerate((sqp, crp)):
            line = jnp.sum((part[0, j] + part[1, j]).T, axis=0, keepdims=True)
            for k in range(2):
                half = line[:, k * HEAD_DIM : (k + 1) * HEAD_DIM]
                tile = jnp.where(which == n * 4 + core * 2 + k, half, tile)
    slot = x * 2 + c
    xb[pl.ds(slot, 1)] = tile[None]
    for peer in peers:
        pltpu.make_async_remote_copy(
            src_ref=xb.at[slot],
            dst_ref=xb.at[slot],
            send_sem=x_s,
            recv_sem=x_r,
            device_id=peer,
            device_id_type=MESH,
        ).start()
    bytes_of(xb, len(peers), x_r)
    total = xb[0]
    for n in range(1, 2 * XS):
        total = total + xb[n]
    width = HEADS * HEAD_DIM
    meansq = total[0:4] / width + EPSILON
    cross = total[4:8] / width
    tot[0:4] = lax.rsqrt(meansq)
    tot[4:8] = cross / meansq
    for j, core in enumerate((c, oc)):
        for k in range(2):
            rows = pl.ds(k * HEAD_DIM, HEAD_DIM)
            for n, out in enumerate((rr, co)):
                line = tot[pl.ds(n * 4 + core * 2 + k, 1), :]
                out[j, rows] = jnp.broadcast_to(line, (HEAD_DIM, HEAD_DIM)).T

    gives = [pair_copy(yd.at[g], rd.at[g], yd_s.at[g], yd_r.at[g]) for g in range(GROUPS)]
    for g in range(GROUPS):
        parts = []
        for r in range(GH):
            at = g * GH + r
            pair = []
            for j in range(2):
                d = rr[j] * (xsc[j, at] - xat[j, at] * co[j])
                d = d.astype(bf16)
                if j == 0:
                    dat[c * HALF + at] = d
                else:
                    yd[g, r] = d.astype(f32)
                pair.append(nn(qft[j, at], d))
            even = jnp.where(c == 0, pair[0], pair[1])
            odd = jnp.where(c == 0, pair[1], pair[0])
            hodd[g, rows_of(r)] = odd
            parts.append(even + keep_even * odd)
        pbuf[GROUPS + g] = jnp.concatenate(parts, axis=0).reshape(CHIPS, SL, HEAD_DIM)
        forward(GROUPS + g)
        gives[g].start()

    def near_bwd(h, state):
        dp = (nt(dat[h], vh[h]) * mask[...]).astype(bf16)
        dpt = (nt(vh[h], dat[h]) * mask_t[...]).astype(bf16)
        dq = nn(dp, kh[h]) + first_m[...] * nt(dat[h], state)
        tmp[pl.ds(h, TOK, stride=LH), :] = dq
        dkp[h] = nn(dpt, qh[h])
        dvp[h] = nn(probs_t[h], dat[h])

    for r in range(HALF):
        near_bwd(c * HALF + r, st[0, r])
    for g in range(GROUPS):
        turn(GROUPS + g, True)
    for g in range(GROUPS):
        pair_copy(snd.at[g], stb.at[g], back_s.at[g], back_r.at[g]).wait_recv()
        gives[g].wait_recv()
        for r in range(GH):
            h = oc * HALF + g * GH + r
            dat[h] = rd[g, r].astype(bf16)
            near_bwd(h, stb[g, rows_of(r)].astype(bf16))
    oq[...] = tmp[...].reshape(TOK, LH, HEAD_DIM).astype(bf16)

    def last_of(h, state):
        at = pl.ds(h, TOK, stride=LH)
        tk[at, :] = dkp[h] + last_m[...] * nt(vh[h], state)
        tv[at, :] = dvp[h] + last_m[...] * nn(kh[h], state)

    def own_last(g):
        own = split(GROUPS + g, 1, hodd[g], keep_odd).astype(bf16)
        for r in range(GH):
            last_of(c * HALF + g * GH + r, own[r * HEAD_DIM : (r + 1) * HEAD_DIM])

    def other_last(g):
        i = GROUPS + g

        @pl.when(jnp.logical_or(c == 0, m >= EARLY))
        def _():
            pair_copy(snd.at[i], stb.at[i], back_s.at[i], back_r.at[i]).wait_recv()

        @pl.when(jnp.logical_and(c == 1, m < EARLY))
        def _():
            bytes_of(direct.at[g], CHIPS, dir_r.at[g])
            stb[i] = direct[g].reshape(ROWS, HEAD_DIM)

        for r in range(GH):
            last_of(oc * HALF + g * GH + r, stb[i, rows_of(r)].astype(bf16))

    own_last(0)
    own_last(1)
    other_last(0)
    other_last(1)

    bytes_of(xb, len(peers), x_s)
    for swap in swaps:
        swap.wait_send()
    for g in range(GROUPS):
        firsts[g].wait_send()
        gives[g].wait_send()
    for g in range(GROUPS):
        pair_copy(snd.at[g], stb.at[g], back_s.at[g], back_r.at[g]).wait_send()

        @pl.when(c == 0)
        def _(g=g):
            bytes_of(direct.at[g], EARLY, dir_s.at[g])

        @pl.when(jnp.logical_or(c == 1, m >= EARLY))
        def _(i=GROUPS + g):
            pair_copy(snd.at[i], stb.at[i], back_s.at[i], back_r.at[i]).wait_send()

    for i in range(2 * GROUPS):
        bytes_of(fr.at[i], CHIPS - 1, fwd_s.at[i])
        bytes_of(sbuf.at[i], CHIPS - 1, ret_s.at[i])


def finish(oq, tk, tv, out_q, out_k, out_v, buf, sem):
    pltpu.make_async_copy(oq, out_q, sem.at[0]).start()
    for n, (src, dst) in enumerate(((tk, out_k), (tv, out_v))):
        for p in range(PIECES):
            rows = pl.ds(p * TOK // PIECES, TOK // PIECES)
            flat = pl.ds(p * TOK * LH // PIECES, TOK * LH // PIECES)
            buf[n, rows] = src[flat, :].reshape(TOK // PIECES, LH, HEAD_DIM).astype(bf16)
            pltpu.make_async_copy(buf.at[n, rows], dst.at[rows], sem.at[1 + n * PIECES + p]).start()
    pltpu.make_async_copy(oq, out_q, sem.at[0]).wait()
    for n, dst in enumerate((out_k, out_v)):
        for p in range(PIECES):
            rows = pl.ds(p * TOK // PIECES, TOK // PIECES)
            pltpu.make_async_copy(buf.at[n, rows], dst.at[rows], sem.at[1 + n * PIECES + p]).wait()


def local(queries, keys, values, out_grad, gain, starts):
    vm = pl.BlockSpec(memory_space=pltpu.VMEM)
    hb = pl.BlockSpec(memory_space=pltpu.HBM)
    args = [
        pltpu.with_memory_space_constraint(a, pltpu.HBM)
        for a in (starts, gain, queries, keys, values, out_grad)
    ]
    flat = jax.ShapeDtypeStruct((TOK * LH, HEAD_DIM), f32)
    out = jax.ShapeDtypeStruct((TOK, LH, HEAD_DIM), bf16)
    V = pltpu.VMEM
    D = pltpu.SemaphoreType.DMA
    N = 2 * GROUPS
    heads16 = V((LH, TOK, HEAD_DIM), bf16)
    heads32 = V((LH, TOK, HEAD_DIM), f32)
    cols = V((TOK, HEAD_DIM), f32)
    half32 = V((HALF, TOK, HEAD_DIM), f32)
    both32 = V((2, HALF, TOK, HEAD_DIM), f32)
    part = V((GROUPS, ROWS, HEAD_DIM), f32)
    parts2 = V((N, ROWS, HEAD_DIM), f32)
    slices = V((N, CHIPS, SL, HEAD_DIM), f32)
    parts = pl.pallas_call(
        kernel,
        out_shape=(out, flat, flat),
        in_specs=[hb] * 6,
        out_specs=(vm, vm, vm),
        scratch_shapes=[
            pltpu.SMEM((4,), jnp.int32),
            V((LH, HEAD_DIM), f32),
            V((4, TOK, LH, HEAD_DIM), bf16),
            V((TOK * LH, HEAD_DIM), f32),
            heads16,
            heads16,
            heads16,
            heads32,
            V((TOK, TOK), f32),
            V((TOK, TOK), f32),
            cols,
            cols,
            V((LH, TOK, TOK), bf16),
            heads16,
            heads32,
            heads32,
            both32,
            both32,
            both32,
            half32,
            half32,
            half32,
            half32,
            V((GROUPS, GH, TOK, HEAD_DIM), f32),
            V((GROUPS, GH, TOK, HEAD_DIM), f32),
            V((2, HALF, TOK, HEAD_DIM), bf16),
            V((2, HALF, HEAD_DIM, TOK), bf16),
            V((2, HALF, HEAD_DIM, HEAD_DIM), bf16),
            V((GROUPS, 2, TOK, HEAD_DIM), f32),
            V((GROUPS, 2, TOK, HEAD_DIM), f32),
            V((2, TOK, HEAD_DIM), f32),
            V((2, TOK, HEAD_DIM), f32),
            V((CHIPS, SL, HEAD_DIM), f32),
            part,
            part,
            part,
            part,
            slices,
            slices,
            slices,
            slices,
            V((GROUPS, CHIPS, SL, HEAD_DIM), f32),
            parts2,
            parts2,
            V((2 * XS, 8, HEAD_DIM), f32),
            V((8, HEAD_DIM), f32),
            D((6,)),
            D((GROUPS,)),
            D((GROUPS,)),
            D((N,)),
            D((N,)),
            D((N,)),
            D((N,)),
            D((GROUPS,)),
            D((GROUPS,)),
            D((N,)),
            D((N,)),
            D((3,)),
            D((3,)),
            D((GROUPS,)),
            D((GROUPS,)),
            D,
            D,
            pltpu.SemaphoreType.REGULAR,
            pltpu.SemaphoreType.REGULAR,
        ],
        compiler_params=pltpu.CompilerParams(
            collective_id=0, has_side_effects=True, vmem_limit_bytes=32 * 2**20
        ),
        cost_estimate=pl.CostEstimate(
            flops=1_400_000_000, bytes_accessed=4_000_000, transcendentals=2048
        ),
        name="fused",
    )(*args)
    return pl.pallas_call(
        finish,
        out_shape=(out, out, out),
        in_specs=[vm] * 3,
        out_specs=(hb, hb, hb),
        scratch_shapes=[V((2, TOK, LH, HEAD_DIM), bf16), D((1 + 2 * PIECES,))],
        compiler_params=pltpu.CompilerParams(vmem_limit_bytes=4 * 2**20),
        name="finish",
    )(*parts)


def solution(mesh):
    spec = P("ctx", "head", None)
    return jax.shard_map(
        local,
        mesh=mesh,
        in_specs=(spec, spec, spec, spec, P("head", None), P()),
        out_specs=(spec, spec, spec),
        check_vma=False,
    )
```

```python
import jax
import jax.numpy as jnp
from jax import lax
from jax.experimental import pallas as pl
from jax.experimental.pallas import tpu as pltpu
from jax.sharding import PartitionSpec as P

HEADS = 32
HEAD_DIM = 128
EPSILON = 1e-06
ZS, YS, XS = 8, 4, 4
CHIPS = ZS * YS
TOK = 256
LH = 8
HALF = 4
GROUPS = 2
GH = HALF // GROUPS
ROWS = GH * HEAD_DIM
SL = ROWS // CHIPS
CHUNK = 64
EARLY = 1
PIECES = 4
FAR = sorted(
    ((dz, dy) for dz in range(ZS) for dy in range(YS) if dz or dy),
    key=lambda o: (-min(o[0], ZS - o[0]), -min(o[1], YS - o[1])),
)
def reach(o):
    z = min(o[0], ZS - o[0])
    y = min(o[1], YS - o[1])
    return 0.43 * z + 0.15 * y + (0.55 if z and y else 0.0)


ORDER = sorted(FAR, key=lambda o: -reach(o))
MESH = pl.DeviceIdType.MESH
f32 = jnp.float32
bf16 = jnp.bfloat16


def nt(a, b):
    return lax.dot_general(a, b, (((1,), (1,)), ((), ())), preferred_element_type=f32)


def nn(a, b):
    return lax.dot_general(a, b, (((1,), (0,)), ((), ())), preferred_element_type=f32)


def tn(a, b):
    return lax.dot_general(a, b, (((0,), (0,)), ((), ())), preferred_element_type=f32)


def kernel(
    starts_in, gain_in, q_in, k_in, v_in, g_in, oq, tk, tv,
    starts, gain, raw, tmp, qh, kh, vh, sc, mask, mask_t, first_m, last_m, probs_t, dat, dkp, dvp,
    xin, xat, xsc, yin, ysc, yq, rq, yd, rd, xq, qft, st,
    sqp, crp, rr, co, keeps, tme, toth, tsib, hodd, pbuf, fr, pb, sbuf, direct, snd, stb, xb, tot,
    in_sem, pair_s, pair_r, fwd_s, fwd_r, ret_s, ret_r, dir_s, dir_r, back_s, back_r, ex_s, ex_r, yd_s, yd_r, x_s, x_r, hello, go,
):
    b = lax.axis_index("ctx")
    x = lax.axis_index("head")
    c = lax.rem(b, 2)
    m = b // 2
    mz = m // YS
    my = lax.rem(m, YS)
    oc = 1 - c
    sib = {"ctx": m * 2 + oc, "head": x}

    def chip(t):
        return {"ctx": t * 2 + c, "head": x}

    loads = [
        pltpu.make_async_copy(src, dst, in_sem.at[n])
        for n, (src, dst) in enumerate(
            (
                (starts_in, starts),
                (k_in, raw.at[0]),
                (v_in, raw.at[1]),
                (q_in, raw.at[2]),
                (g_in, raw.at[3]),
                (gain_in, gain),
            )
        )
    ]

    def others(n, order=FAR):
        return lax.rem(mz + order[n][0], ZS) * YS + lax.rem(my + order[n][1], YS)

    peers = [
        {"ctx": m * 2 + lax.rem(c + e, 2), "head": lax.rem(x + d, XS)}
        for d in (2, 1, 3, 0)
        for e in (1, 0)
        if (d, e) != (0, 0)
    ]
    bar = pltpu.get_barrier_semaphore()

    @pl.when(c == 1)
    def _():
        pl.semaphore_signal(bar, inc=1, device_id=sib, device_id_type=MESH)

    for n in range(CHIPS - 1):
        far = {"ctx": others(n) * 2 + 1, "head": x}
        pl.semaphore_signal(bar, inc=1, device_id=far, device_id_type=MESH)
    for d in (2, 1, 3):
        side = {"ctx": m * 2 + 1, "head": lax.rem(x + d, XS)}
        pl.semaphore_signal(bar, inc=1, device_id=side, device_id_type=MESH)
    for load in loads:
        load.start()

    @pl.when(c == 0)
    def _():
        pl.semaphore_wait(bar, 1)
        pl.semaphore_signal(hello, inc=1, device_id=sib, device_id_type=MESH)

    loads[0].wait()
    sv = [starts[n] for n in range(4)]

    def seg_of(pos):
        total = (pos >= sv[0]).astype(jnp.int32)
        for n in range(1, 4):
            total = total + (pos >= sv[n]).astype(jnp.int32)
        return total

    def keep(lo, size):
        hit = (sv[0] >= lo) & (sv[0] < lo + size)
        for n in range(1, 4):
            hit = hit | ((sv[n] >= lo) & (sv[n] < lo + size))
        return jnp.where(hit, 0.0, 1.0).astype(f32)

    base = b * TOK
    row_c = lax.broadcasted_iota(jnp.int32, (TOK, HEAD_DIM), 0) + base
    seg_c = seg_of(row_c)
    begins0 = (base == sv[0]) | (base == sv[1]) | (base == sv[2]) | (base == sv[3])
    seg0 = jnp.where(begins0, -1, seg_of(base))
    first_m[...] = (seg_c == seg0).astype(f32)
    last_m[...] = (seg_c == seg_of(base + TOK - 1)).astype(f32)
    keep_even = keep(2 * m * TOK, TOK)
    keep_odd = keep((2 * m + 1) * TOK, TOK)

    def relayout(n, out, tmp):
        tmp[...] = raw[n].astype(f32).reshape(TOK * LH, HEAD_DIM)
        for h in range(LH):
            out[h] = tmp[pl.ds(h, TOK, stride=LH), :].astype(out.dtype)

    def pair_copy(src, dst, ss, rs):
        return pltpu.make_async_remote_copy(
            src_ref=src, dst_ref=dst, send_sem=ss, recv_sem=rs, device_id=sib, device_id_type=MESH
        )

    def slice_copy(src, dst, ss, rs, t, core):
        return pltpu.make_async_remote_copy(
            src_ref=src.at[t],
            dst_ref=dst.at[m],
            send_sem=ss,
            recv_sem=rs,
            device_id={"ctx": t * 2 + core, "head": x},
            device_id_type=MESH,
        )

    def send_out(out, groups):
        src, dst, ss, rs = out
        for i in groups:
            for n in range(CHIPS - 1):
                slice_copy(src.at[i], dst.at[i], ss.at[i], rs.at[i], others(n, ORDER), c).start()

    def bytes_of(buf, count, sem):
        part = buf.at[pl.ds(0, count)]
        pltpu.make_async_copy(part, part, sem).wait()

    def rows_of(r):
        return pl.ds(r * HEAD_DIM, HEAD_DIM)

    going = (pbuf, fr, fwd_s, fwd_r)
    coming = (pb, sbuf, ret_s, ret_r)

    def turn(i, reverse):
        bytes_of(fr.at[i], CHIPS - 1, fwd_r.at[i])
        carry = jnp.zeros((SL, HEAD_DIM), f32)
        for n in range(CHIPS):
            t = CHIPS - 1 - n if reverse else n
            pb[i, t] = carry
            carry = fr[i, t] + keeps[t] * carry
        if reverse:
            g = i - GROUPS

            @pl.when(c == 0)
            def _():
                for t in range(EARLY):
                    slice_copy(pb.at[i], direct.at[g], dir_s.at[g], dir_r.at[g], t, 1).start()

        send_out(coming, (i,))
        sbuf[i, pl.ds(m, 1)] = pb[i, pl.ds(m, 1)]

    def split(i, edge, part, weight):
        bytes_of(sbuf.at[i], CHIPS - 1, ret_r.at[i])
        whole = sbuf[i].reshape(ROWS, HEAD_DIM)
        away = part + weight * whole
        is_edge = c == edge
        snd[i] = jnp.where(is_edge, away, whole)

        @pl.when(jnp.logical_or(edge == 0, jnp.logical_or(c == 1, m >= EARLY)))
        def _():
            pair_copy(snd.at[i], stb.at[i], back_s.at[i], back_r.at[i]).start()

        return jnp.where(is_edge, whole, away)

    loads[1].wait()
    relayout(0, kh, tk)
    loads[2].wait()
    relayout(1, vh, tv)

    def tail_of(h):
        return tn((kh[h].astype(f32) * last_m[...]).astype(bf16), vh[h])

    firsts = [pair_copy(toth.at[g], tsib.at[g], pair_s.at[g], pair_r.at[g]) for g in range(GROUPS)]
    for g in range(GROUPS):
        for r in range(GH):
            toth[g, rows_of(r)] = tail_of(oc * HALF + g * GH + r)
        if g == 0:

            @pl.when(c == 1)
            def _():
                pl.semaphore_wait(hello, 1)

        firsts[g].start()
    for g in range(GROUPS):
        for r in range(GH):
            tme[g, rows_of(r)] = tail_of(c * HALF + g * GH + r)
    one = jnp.ones((), f32)
    w_me = jnp.where(c == 0, keep_odd, one)
    w_sib = jnp.where(c == 0, one, keep_odd)
    for g in range(GROUPS):
        firsts[g].wait_recv()
        pbuf[g] = (tme[g] * w_me + tsib[g] * w_sib).reshape(CHIPS, SL, HEAD_DIM)

    @pl.when(c == 1)
    def _():
        pl.semaphore_wait(bar, 2 * (CHIPS - 1) + 2 * (XS - 1))
        pl.semaphore_signal(go, inc=1, device_id=sib, device_id_type=MESH)

    @pl.when(c == 0)
    def _():
        pl.semaphore_wait(go, 1)

    first = range(GROUPS)
    second = range(GROUPS, 2 * GROUPS)
    send_out(going, first)
    for g in first:
        fr[g, pl.ds(m, 1)] = pbuf[g, pl.ds(m, 1)]
    chip_row = lax.broadcasted_iota(jnp.int32, (CHIPS, SL, HEAD_DIM), 0)
    keeps[...] = keep(chip_row * (2 * TOK), 2 * TOK)
    loads[3].wait()
    relayout(2, qh, tk)
    ri = lax.broadcasted_iota(jnp.int32, (TOK, TOK), 0)
    ci = lax.broadcasted_iota(jnp.int32, (TOK, TOK), 1)
    same = seg_of(ri + base) == seg_of(ci + base)
    mask[...] = ((ri >= ci) & same).astype(f32)
    mask_t[...] = ((ri <= ci) & same).astype(f32)

    def near_fwd(h):
        p = (nt(qh[h], kh[h]) * mask[...]).astype(bf16)
        probs_t[h] = (nt(kh[h], qh[h]) * mask_t[...]).astype(bf16)
        return nn(p, vh[h])

    swaps = [
        pair_copy(src, dst, ex_s.at[n], ex_r.at[n])
        for n, (src, dst) in enumerate(((yin, xin.at[1]), (yq, rq), (ysc, xsc.at[1])))
    ]
    for r in range(HALF):
        h = oc * HALF + r
        yq[r] = qh[h].astype(f32) * first_m[...]
        yin[r] = near_fwd(h)
    swaps[0].start()
    swaps[1].start()
    turn(0, False)
    turn(1, False)
    loads[4].wait()
    loads[5].wait()
    relayout(3, sc, tv)
    for r in range(HALF):
        ysc[r] = sc[oc * HALF + r] * gain[pl.ds(oc * HALF + r, 1), :]
    swaps[2].start()
    for r in range(HALF):
        h = c * HALF + r
        xsc[0, r] = sc[h] * gain[pl.ds(h, 1), :]
        masked = qh[h].astype(f32) * first_m[...]
        xq[0, r] = masked.astype(bf16)
        qft[0, r] = masked.T.astype(bf16)
        xin[0, r] = near_fwd(h)
    swaps[1].wait_recv()
    for r in range(HALF):
        xq[1, r] = rq[r].astype(bf16)
        qft[1, r] = rq[r].T.astype(bf16)
    swaps[0].wait_recv()
    swaps[2].wait_recv()

    for g in range(GROUPS):
        own = split(g, 0, jnp.where(c == 0, tme[g], tsib[g]), keep_even)
        st[0, g * GH : (g + 1) * GH] = own.astype(bf16).reshape(GH, HEAD_DIM, HEAD_DIM)
        st[1, g * GH : (g + 1) * GH] = snd[g].astype(bf16).reshape(GH, HEAD_DIM, HEAD_DIM)
        for j in range(2):
            for lo in range(0, TOK, CHUNK):
                rows = pl.ds(lo, CHUNK)
                sq = jnp.zeros((CHUNK, HEAD_DIM), f32)
                cr = jnp.zeros((CHUNK, HEAD_DIM), f32)
                for r in range(g * GH, (g + 1) * GH):
                    a = xin[j, r, rows] + nn(xq[j, r, rows], st[j, r])
                    xat[j, r, rows] = a
                    sq = sq + a * a
                    cr = cr + a * xsc[j, r, rows]
                sqp[g, j, rows] = sq
                crp[g, j, rows] = cr

    which = lax.broadcasted_iota(jnp.int32, (8, HEAD_DIM), 0)
    tile = jnp.zeros((8, HEAD_DIM), f32)
    for j, core in enumerate((c, oc)):
        for n, part in enumerate((sqp, crp)):
            line = jnp.sum((part[0, j] + part[1, j]).T, axis=0, keepdims=True)
            for k in range(2):
                half = line[:, k * HEAD_DIM : (k + 1) * HEAD_DIM]
                tile = jnp.where(which == n * 4 + core * 2 + k, half, tile)
    slot = x * 2 + c
    xb[pl.ds(slot, 1)] = tile[None]
    for peer in peers:
        pltpu.make_async_remote_copy(
            src_ref=xb.at[slot],
            dst_ref=xb.at[slot],
            send_sem=x_s,
            recv_sem=x_r,
            device_id=peer,
            device_id_type=MESH,
        ).start()
    bytes_of(xb, len(peers), x_r)
    total = xb[0]
    for n in range(1, 2 * XS):
        total = total + xb[n]
    width = HEADS * HEAD_DIM
    meansq = total[0:4] / width + EPSILON
    cross = total[4:8] / width
    tot[0:4] = lax.rsqrt(meansq)
    tot[4:8] = cross / meansq
    for j, core in enumerate((c, oc)):
        for k in range(2):
            rows = pl.ds(k * HEAD_DIM, HEAD_DIM)
            for n, out in enumerate((rr, co)):
                line = tot[pl.ds(n * 4 + core * 2 + k, 1), :]
                out[j, rows] = jnp.broadcast_to(line, (HEAD_DIM, HEAD_DIM)).T

    gives = [pair_copy(yd.at[g], rd.at[g], yd_s.at[g], yd_r.at[g]) for g in range(GROUPS)]
    for g in range(GROUPS):
        parts = []
        for r in range(GH):
            at = g * GH + r
            pair = []
            for j in range(2):
                d = rr[j] * (xsc[j, at] - xat[j, at] * co[j])
                d = d.astype(bf16)
                if j == 0:
                    dat[c * HALF + at] = d
                else:
                    yd[g, r] = d.astype(f32)
                pair.append(nn(qft[j, at], d))
            even = jnp.where(c == 0, pair[0], pair[1])
            odd = jnp.where(c == 0, pair[1], pair[0])
            hodd[g, rows_of(r)] = odd
            parts.append(even + keep_even * odd)
        pbuf[GROUPS + g] = jnp.concatenate(parts, axis=0).reshape(CHIPS, SL, HEAD_DIM)
        fr[GROUPS + g, pl.ds(m, 1)] = pbuf[GROUPS + g, pl.ds(m, 1)]
        send_out(going, (GROUPS + g,))
        gives[g].start()

    def near_bwd(h, state):
        dp = (nt(dat[h], vh[h]) * mask[...]).astype(bf16)
        dpt = (nt(vh[h], dat[h]) * mask_t[...]).astype(bf16)
        dq = nn(dp, kh[h]) + first_m[...] * nt(dat[h], state)
        tmp[pl.ds(h, TOK, stride=LH), :] = dq
        dkp[h] = nn(dpt, qh[h])
        dvp[h] = nn(probs_t[h], dat[h])

    for r in range(HALF):
        near_bwd(c * HALF + r, st[0, r])
    for i in second:
        turn(i, True)
    for g in range(GROUPS):
        pair_copy(snd.at[g], stb.at[g], back_s.at[g], back_r.at[g]).wait_recv()
        gives[g].wait_recv()
        for r in range(GH):
            h = oc * HALF + g * GH + r
            dat[h] = rd[g, r].astype(bf16)
            near_bwd(h, stb[g, rows_of(r)].astype(bf16))
    oq[...] = tmp[...].reshape(TOK, LH, HEAD_DIM).astype(bf16)

    def last_of(h, state):
        at = pl.ds(h, TOK, stride=LH)
        tk[at, :] = dkp[h] + last_m[...] * nt(vh[h], state)
        tv[at, :] = dvp[h] + last_m[...] * nn(kh[h], state)

    def own_last(g):
        own = split(GROUPS + g, 1, hodd[g], keep_odd).astype(bf16)
        for r in range(GH):
            last_of(c * HALF + g * GH + r, own[r * HEAD_DIM : (r + 1) * HEAD_DIM])

    def other_last(g):
        i = GROUPS + g

        @pl.when(jnp.logical_or(c == 0, m >= EARLY))
        def _():
            pair_copy(snd.at[i], stb.at[i], back_s.at[i], back_r.at[i]).wait_recv()

        @pl.when(jnp.logical_and(c == 1, m < EARLY))
        def _():
            bytes_of(direct.at[g], CHIPS, dir_r.at[g])
            stb[i] = direct[g].reshape(ROWS, HEAD_DIM)

        for r in range(GH):
            last_of(oc * HALF + g * GH + r, stb[i, rows_of(r)].astype(bf16))

    own_last(0)
    own_last(1)
    other_last(0)
    other_last(1)

    bytes_of(xb, len(peers), x_s)
    for swap in swaps:
        swap.wait_send()
    for g in range(GROUPS):
        firsts[g].wait_send()
        gives[g].wait_send()
    for g in range(GROUPS):
        pair_copy(snd.at[g], stb.at[g], back_s.at[g], back_r.at[g]).wait_send()

        @pl.when(c == 0)
        def _(g=g):
            bytes_of(direct.at[g], EARLY, dir_s.at[g])

        @pl.when(jnp.logical_or(c == 1, m >= EARLY))
        def _(i=GROUPS + g):
            pair_copy(snd.at[i], stb.at[i], back_s.at[i], back_r.at[i]).wait_send()

    for i in range(2 * GROUPS):
        bytes_of(fr.at[i], CHIPS - 1, fwd_s.at[i])
        bytes_of(sbuf.at[i], CHIPS - 1, ret_s.at[i])


def finish(oq, tk, tv, out_q, out_k, out_v, buf, sem):
    pltpu.make_async_copy(oq, out_q, sem.at[0]).start()
    for n, (src, dst) in enumerate(((tk, out_k), (tv, out_v))):
        for p in range(PIECES):
            rows = pl.ds(p * TOK // PIECES, TOK // PIECES)
            flat = pl.ds(p * TOK * LH // PIECES, TOK * LH // PIECES)
            buf[n, rows] = src[flat, :].reshape(TOK // PIECES, LH, HEAD_DIM).astype(bf16)
            pltpu.make_async_copy(buf.at[n, rows], dst.at[rows], sem.at[1 + n * PIECES + p]).start()
    pltpu.make_async_copy(oq, out_q, sem.at[0]).wait()
    for n, dst in enumerate((out_k, out_v)):
        for p in range(PIECES):
            rows = pl.ds(p * TOK // PIECES, TOK // PIECES)
            pltpu.make_async_copy(buf.at[n, rows], dst.at[rows], sem.at[1 + n * PIECES + p]).wait()


def local(queries, keys, values, out_grad, gain, starts):
    vm = pl.BlockSpec(memory_space=pltpu.VMEM)
    hb = pl.BlockSpec(memory_space=pltpu.HBM)
    args = [
        pltpu.with_memory_space_constraint(a, pltpu.HBM)
        for a in (starts, gain, queries, keys, values, out_grad)
    ]
    flat = jax.ShapeDtypeStruct((TOK * LH, HEAD_DIM), f32)
    out = jax.ShapeDtypeStruct((TOK, LH, HEAD_DIM), bf16)
    V = pltpu.VMEM
    D = pltpu.SemaphoreType.DMA
    N = 2 * GROUPS
    heads16 = V((LH, TOK, HEAD_DIM), bf16)
    heads32 = V((LH, TOK, HEAD_DIM), f32)
    cols = V((TOK, HEAD_DIM), f32)
    half32 = V((HALF, TOK, HEAD_DIM), f32)
    both32 = V((2, HALF, TOK, HEAD_DIM), f32)
    part = V((GROUPS, ROWS, HEAD_DIM), f32)
    parts2 = V((N, ROWS, HEAD_DIM), f32)
    slices = V((N, CHIPS, SL, HEAD_DIM), f32)
    parts = pl.pallas_call(
        kernel,
        out_shape=(out, flat, flat),
        in_specs=[hb] * 6,
        out_specs=(vm, vm, vm),
        scratch_shapes=[
            pltpu.SMEM((4,), jnp.int32),
            V((LH, HEAD_DIM), f32),
            V((4, TOK, LH, HEAD_DIM), bf16),
            V((TOK * LH, HEAD_DIM), f32),
            heads16,
            heads16,
            heads16,
            heads32,
            V((TOK, TOK), f32),
            V((TOK, TOK), f32),
            cols,
            cols,
            V((LH, TOK, TOK), bf16),
            heads16,
            heads32,
            heads32,
            both32,
            both32,
            both32,
            half32,
            half32,
            half32,
            half32,
            V((GROUPS, GH, TOK, HEAD_DIM), f32),
            V((GROUPS, GH, TOK, HEAD_DIM), f32),
            V((2, HALF, TOK, HEAD_DIM), bf16),
            V((2, HALF, HEAD_DIM, TOK), bf16),
            V((2, HALF, HEAD_DIM, HEAD_DIM), bf16),
            V((GROUPS, 2, TOK, HEAD_DIM), f32),
            V((GROUPS, 2, TOK, HEAD_DIM), f32),
            V((2, TOK, HEAD_DIM), f32),
            V((2, TOK, HEAD_DIM), f32),
            V((CHIPS, SL, HEAD_DIM), f32),
            part,
            part,
            part,
            part,
            slices,
            slices,
            slices,
            slices,
            V((GROUPS, CHIPS, SL, HEAD_DIM), f32),
            parts2,
            parts2,
            V((2 * XS, 8, HEAD_DIM), f32),
            V((8, HEAD_DIM), f32),
            D((6,)),
            D((GROUPS,)),
            D((GROUPS,)),
            D((N,)),
            D((N,)),
            D((N,)),
            D((N,)),
            D((GROUPS,)),
            D((GROUPS,)),
            D((N,)),
            D((N,)),
            D((3,)),
            D((3,)),
            D((GROUPS,)),
            D((GROUPS,)),
            D,
            D,
            pltpu.SemaphoreType.REGULAR,
            pltpu.SemaphoreType.REGULAR,
        ],
        compiler_params=pltpu.CompilerParams(
            collective_id=0, has_side_effects=True, vmem_limit_bytes=32 * 2**20
        ),
        cost_estimate=pl.CostEstimate(
            flops=1_400_000_000, bytes_accessed=4_000_000, transcendentals=2048
        ),
        name="fused",
    )(*args)
    return pl.pallas_call(
        finish,
        out_shape=(out, out, out),
        in_specs=[vm] * 3,
        out_specs=(hb, hb, hb),
        scratch_shapes=[V((2, TOK, LH, HEAD_DIM), bf16), D((1 + 2 * PIECES,))],
        compiler_params=pltpu.CompilerParams(vmem_limit_bytes=4 * 2**20),
        name="finish",
    )(*parts)


def solution(mesh):
    spec = P("ctx", "head", None)
    return jax.shard_map(
        local,
        mesh=mesh,
        in_specs=(spec, spec, spec, spec, P("head", None), P()),
        out_specs=(spec, spec, spec),
        check_vma=False,
    )
```

```python
import jax
import jax.numpy as jnp
from jax import lax
from jax.experimental import pallas as pl
from jax.experimental.pallas import tpu as pltpu
from jax.sharding import PartitionSpec as P

HEADS = 32
HEAD_DIM = 128
EPSILON = 1e-06
ZS, YS, XS = 8, 4, 4
CHIPS = ZS * YS
TOK = 256
LH = 8
HALF = 4
GROUPS = 2
GH = HALF // GROUPS
ROWS = GH * HEAD_DIM
SL = ROWS // CHIPS
CHUNK = 64
EARLY = 1
PIECES = 4
FAR = sorted(
    ((dz, dy) for dz in range(ZS) for dy in range(YS) if dz or dy),
    key=lambda o: (-min(o[0], ZS - o[0]), -min(o[1], YS - o[1])),
)
def reach(o):
    z = min(o[0], ZS - o[0])
    y = min(o[1], YS - o[1])
    return 0.43 * z + 0.4 * y + (0.55 if z and y else 0.0)


ORDER = sorted(FAR, key=lambda o: -reach(o))
MESH = pl.DeviceIdType.MESH
f32 = jnp.float32
bf16 = jnp.bfloat16


def nt(a, b):
    return lax.dot_general(a, b, (((1,), (1,)), ((), ())), preferred_element_type=f32)


def nn(a, b):
    return lax.dot_general(a, b, (((1,), (0,)), ((), ())), preferred_element_type=f32)


def tn(a, b):
    return lax.dot_general(a, b, (((0,), (0,)), ((), ())), preferred_element_type=f32)


def kernel(
    starts_in, gain_in, q_in, k_in, v_in, g_in, oq, tk, tv,
    starts, gain, raw, tmp, qh, kh, vh, sc, mask, mask_t, first_m, last_m, probs_t, dat, dqp, dkp, dvp,
    xin, xat, xsc, yin, ysc, yq, rq, yd, rd, xq, qft, st,
    sqp, crp, rr, co, keeps, tme, toth, tsib, hodd, pbuf, fr, pb, sbuf, direct, snd, stb, xb, tot,
    in_sem, pair_s, pair_r, fwd_s, fwd_r, ret_s, ret_r, dir_s, dir_r, back_s, back_r, ex_s, ex_r, yd_s, yd_r, x_s, x_r, hello, go,
):
    b = lax.axis_index("ctx")
    x = lax.axis_index("head")
    c = lax.rem(b, 2)
    m = b // 2
    mz = m // YS
    my = lax.rem(m, YS)
    oc = 1 - c
    sib = {"ctx": m * 2 + oc, "head": x}

    def chip(t):
        return {"ctx": t * 2 + c, "head": x}

    loads = [
        pltpu.make_async_copy(src, dst, in_sem.at[n])
        for n, (src, dst) in enumerate(
            (
                (starts_in, starts),
                (k_in, raw.at[0]),
                (v_in, raw.at[1]),
                (q_in, raw.at[2]),
                (g_in, raw.at[3]),
                (gain_in, gain),
            )
        )
    ]

    def others(n, order=FAR):
        return lax.rem(mz + order[n][0], ZS) * YS + lax.rem(my + order[n][1], YS)

    peers = [
        {"ctx": m * 2 + lax.rem(c + e, 2), "head": lax.rem(x + d, XS)}
        for d in (2, 1, 3, 0)
        for e in (1, 0)
        if (d, e) != (0, 0)
    ]
    bar = pltpu.get_barrier_semaphore()

    @pl.when(c == 1)
    def _():
        pl.semaphore_signal(bar, inc=1, device_id=sib, device_id_type=MESH)

    for n in range(CHIPS - 1):
        far = {"ctx": others(n, ORDER) * 2 + 1, "head": x}
        pl.semaphore_signal(bar, inc=1, device_id=far, device_id_type=MESH)
    for d in (2, 1, 3):
        side = {"ctx": m * 2 + 1, "head": lax.rem(x + d, XS)}
        pl.semaphore_signal(bar, inc=1, device_id=side, device_id_type=MESH)
    for load in loads:
        load.start()

    @pl.when(c == 0)
    def _():
        pl.semaphore_wait(bar, 1)
        pl.semaphore_signal(hello, inc=1, device_id=sib, device_id_type=MESH)

    loads[0].wait()
    sv = [starts[n] for n in range(4)]

    def seg_of(pos):
        total = (pos >= sv[0]).astype(jnp.int32)
        for n in range(1, 4):
            total = total + (pos >= sv[n]).astype(jnp.int32)
        return total

    def keep(lo, size):
        hit = (sv[0] >= lo) & (sv[0] < lo + size)
        for n in range(1, 4):
            hit = hit | ((sv[n] >= lo) & (sv[n] < lo + size))
        return jnp.where(hit, 0.0, 1.0).astype(f32)

    base = b * TOK
    row_c = lax.broadcasted_iota(jnp.int32, (TOK, HEAD_DIM), 0) + base
    seg_c = seg_of(row_c)
    begins0 = (base == sv[0]) | (base == sv[1]) | (base == sv[2]) | (base == sv[3])
    seg0 = jnp.where(begins0, -1, seg_of(base))
    first_m[...] = (seg_c == seg0).astype(f32)
    last_m[...] = (seg_c == seg_of(base + TOK - 1)).astype(f32)
    keep_even = keep(2 * m * TOK, TOK)
    keep_odd = keep((2 * m + 1) * TOK, TOK)

    def relayout(n, out, tmp):
        tmp[...] = raw[n].astype(f32).reshape(TOK * LH, HEAD_DIM)
        for h in range(LH):
            out[h] = tmp[pl.ds(h, TOK, stride=LH), :].astype(out.dtype)

    def pair_copy(src, dst, ss, rs):
        return pltpu.make_async_remote_copy(
            src_ref=src, dst_ref=dst, send_sem=ss, recv_sem=rs, device_id=sib, device_id_type=MESH
        )

    def slice_copy(src, dst, ss, rs, t, core):
        return pltpu.make_async_remote_copy(
            src_ref=src.at[t],
            dst_ref=dst.at[m],
            send_sem=ss,
            recv_sem=rs,
            device_id={"ctx": t * 2 + core, "head": x},
            device_id_type=MESH,
        )

    def send_out(out, groups):
        src, dst, ss, rs = out
        for i in groups:
            for n in range(CHIPS - 1):
                slice_copy(src.at[i], dst.at[i], ss.at[i], rs.at[i], others(n, ORDER), c).start()

    def bytes_of(buf, count, sem):
        part = buf.at[pl.ds(0, count)]
        pltpu.make_async_copy(part, part, sem).wait()

    def rows_of(r):
        return pl.ds(r * HEAD_DIM, HEAD_DIM)

    going = (pbuf, fr, fwd_s, fwd_r)
    coming = (pb, sbuf, ret_s, ret_r)

    def turn(i, reverse):
        bytes_of(fr.at[i], CHIPS - 1, fwd_r.at[i])
        carry = jnp.zeros((SL, HEAD_DIM), f32)
        for n in range(CHIPS):
            t = CHIPS - 1 - n if reverse else n
            pb[i, t] = carry
            carry = fr[i, t] + keeps[t] * carry
        if reverse:
            g = i - GROUPS

            @pl.when(c == 0)
            def _():
                for t in range(EARLY):
                    slice_copy(pb.at[i], direct.at[g], dir_s.at[g], dir_r.at[g], t, 1).start()

        send_out(coming, (i,))
        sbuf[i, pl.ds(m, 1)] = pb[i, pl.ds(m, 1)]

    def split(i, edge, part, weight):
        bytes_of(sbuf.at[i], CHIPS - 1, ret_r.at[i])
        whole = sbuf[i].reshape(ROWS, HEAD_DIM)
        away = part + weight * whole
        is_edge = c == edge
        snd[i] = jnp.where(is_edge, away, whole)

        @pl.when(jnp.logical_or(edge == 0, jnp.logical_or(c == 1, m >= EARLY)))
        def _():
            pair_copy(snd.at[i], stb.at[i], back_s.at[i], back_r.at[i]).start()

        return jnp.where(is_edge, whole, away)

    loads[1].wait()
    relayout(0, kh, tk)
    loads[2].wait()
    relayout(1, vh, tv)

    def tail_of(h):
        return tn((kh[h].astype(f32) * last_m[...]).astype(bf16), vh[h])

    firsts = [pair_copy(toth.at[g], tsib.at[g], pair_s.at[g], pair_r.at[g]) for g in range(GROUPS)]
    for g in range(GROUPS):
        for r in range(GH):
            toth[g, rows_of(r)] = tail_of(oc * HALF + g * GH + r)
        if g == 0:

            @pl.when(c == 1)
            def _():
                pl.semaphore_wait(hello, 1)

        firsts[g].start()
    for g in range(GROUPS):
        for r in range(GH):
            tme[g, rows_of(r)] = tail_of(c * HALF + g * GH + r)
    one = jnp.ones((), f32)
    w_me = jnp.where(c == 0, keep_odd, one)
    w_sib = jnp.where(c == 0, one, keep_odd)
    for g in range(GROUPS):
        firsts[g].wait_recv()
        pbuf[g] = (tme[g] * w_me + tsib[g] * w_sib).reshape(CHIPS, SL, HEAD_DIM)

    @pl.when(c == 1)
    def _():
        pl.semaphore_wait(bar, 2 * (CHIPS - 1) + 2 * (XS - 1))
        pl.semaphore_signal(go, inc=1, device_id=sib, device_id_type=MESH)

    @pl.when(c == 0)
    def _():
        pl.semaphore_wait(go, 1)

    first = range(GROUPS)
    second = range(GROUPS, 2 * GROUPS)
    send_out(going, first)
    for g in first:
        fr[g, pl.ds(m, 1)] = pbuf[g, pl.ds(m, 1)]
    chip_row = lax.broadcasted_iota(jnp.int32, (CHIPS, SL, HEAD_DIM), 0)
    keeps[...] = keep(chip_row * (2 * TOK), 2 * TOK)
    loads[3].wait()
    relayout(2, qh, tk)
    ri = lax.broadcasted_iota(jnp.int32, (TOK, TOK), 0)
    ci = lax.broadcasted_iota(jnp.int32, (TOK, TOK), 1)
    same = seg_of(ri + base) == seg_of(ci + base)
    mask[...] = ((ri >= ci) & same).astype(f32)
    mask_t[...] = ((ri <= ci) & same).astype(f32)

    def near_fwd(h):
        p = (nt(qh[h], kh[h]) * mask[...]).astype(bf16)
        probs_t[h] = (nt(kh[h], qh[h]) * mask_t[...]).astype(bf16)
        return nn(p, vh[h])

    swaps = [
        pair_copy(src, dst, ex_s.at[n], ex_r.at[n])
        for n, (src, dst) in enumerate(((yin, xin.at[1]), (yq, rq), (ysc, xsc.at[1])))
    ]
    for r in range(HALF):
        h = oc * HALF + r
        yq[r] = qh[h].astype(f32) * first_m[...]
        yin[r] = near_fwd(h)
    swaps[0].start()
    swaps[1].start()
    turn(0, False)
    turn(1, False)
    loads[4].wait()
    loads[5].wait()
    relayout(3, sc, tv)
    for r in range(HALF):
        ysc[r] = sc[oc * HALF + r] * gain[pl.ds(oc * HALF + r, 1), :]
    swaps[2].start()
    for r in range(HALF):
        h = c * HALF + r
        xsc[0, r] = sc[h] * gain[pl.ds(h, 1), :]
        masked = qh[h].astype(f32) * first_m[...]
        xq[0, r] = masked.astype(bf16)
        qft[0, r] = masked.T.astype(bf16)
        xin[0, r] = near_fwd(h)
    swaps[1].wait_recv()
    for r in range(HALF):
        xq[1, r] = rq[r].astype(bf16)
        qft[1, r] = rq[r].T.astype(bf16)
    swaps[0].wait_recv()
    swaps[2].wait_recv()

    for g in range(GROUPS):
        own = split(g, 0, jnp.where(c == 0, tme[g], tsib[g]), keep_even)
        st[0, g * GH : (g + 1) * GH] = own.astype(bf16).reshape(GH, HEAD_DIM, HEAD_DIM)
        st[1, g * GH : (g + 1) * GH] = snd[g].astype(bf16).reshape(GH, HEAD_DIM, HEAD_DIM)
        for j in range(2):
            for lo in range(0, TOK, CHUNK):
                rows = pl.ds(lo, CHUNK)
                sq = jnp.zeros((CHUNK, HEAD_DIM), f32)
                cr = jnp.zeros((CHUNK, HEAD_DIM), f32)
                for r in range(g * GH, (g + 1) * GH):
                    a = xin[j, r, rows] + nn(xq[j, r, rows], st[j, r])
                    xat[j, r, rows] = a
                    sq = sq + a * a
                    cr = cr + a * xsc[j, r, rows]
                sqp[g, j, rows] = sq
                crp[g, j, rows] = cr

    which = lax.broadcasted_iota(jnp.int32, (8, HEAD_DIM), 0)
    tile = jnp.zeros((8, HEAD_DIM), f32)
    for j, core in enumerate((c, oc)):
        for n, part in enumerate((sqp, crp)):
            line = jnp.sum((part[0, j] + part[1, j]).T, axis=0, keepdims=True)
            for k in range(2):
                half = line[:, k * HEAD_DIM : (k + 1) * HEAD_DIM]
                tile = jnp.where(which == n * 4 + core * 2 + k, half, tile)
    slot = x * 2 + c
    xb[pl.ds(slot, 1)] = tile[None]
    for peer in peers:
        pltpu.make_async_remote_copy(
            src_ref=xb.at[slot],
            dst_ref=xb.at[slot],
            send_sem=x_s,
            recv_sem=x_r,
            device_id=peer,
            device_id_type=MESH,
        ).start()
    bytes_of(xb, len(peers), x_r)
    total = xb[0]
    for n in range(1, 2 * XS):
        total = total + xb[n]
    width = HEADS * HEAD_DIM
    meansq = total[0:4] / width + EPSILON
    cross = total[4:8] / width
    tot[0:4] = lax.rsqrt(meansq)
    tot[4:8] = cross / meansq
    for j, core in enumerate((c, oc)):
        for k in range(2):
            rows = pl.ds(k * HEAD_DIM, HEAD_DIM)
            for n, out in enumerate((rr, co)):
                line = tot[pl.ds(n * 4 + core * 2 + k, 1), :]
                out[j, rows] = jnp.broadcast_to(line, (HEAD_DIM, HEAD_DIM)).T

    gives = [pair_copy(yd.at[g], rd.at[g], yd_s.at[g], yd_r.at[g]) for g in range(GROUPS)]
    for g in range(GROUPS):
        parts = []
        for r in range(GH):
            at = g * GH + r
            pair = []
            for j in range(2):
                d = rr[j] * (xsc[j, at] - xat[j, at] * co[j])
                d = d.astype(bf16)
                if j == 0:
                    dat[c * HALF + at] = d
                else:
                    yd[g, r] = d.astype(f32)
                pair.append(nn(qft[j, at], d))
            even = jnp.where(c == 0, pair[0], pair[1])
            odd = jnp.where(c == 0, pair[1], pair[0])
            hodd[g, rows_of(r)] = odd
            parts.append(even + keep_even * odd)
        pbuf[GROUPS + g] = jnp.concatenate(parts, axis=0).reshape(CHIPS, SL, HEAD_DIM)
        fr[GROUPS + g, pl.ds(m, 1)] = pbuf[GROUPS + g, pl.ds(m, 1)]
        send_out(going, (GROUPS + g,))
        gives[g].start()

    def near_bwd(h, state):
        dp = (nt(dat[h], vh[h]) * mask[...]).astype(bf16)
        dpt = (nt(vh[h], dat[h]) * mask_t[...]).astype(bf16)
        dq = nn(dp, kh[h]) + first_m[...] * nt(dat[h], state)
        dqp[h] = dq
        dkp[h] = nn(dpt, qh[h])
        dvp[h] = nn(probs_t[h], dat[h])

    for r in range(HALF):
        near_bwd(c * HALF + r, st[0, r])
    for i in second:
        turn(i, True)
    for g in range(GROUPS):
        pair_copy(snd.at[g], stb.at[g], back_s.at[g], back_r.at[g]).wait_recv()
        gives[g].wait_recv()
        for r in range(GH):
            h = oc * HALF + g * GH + r
            dat[h] = rd[g, r].astype(bf16)
            near_bwd(h, stb[g, rows_of(r)].astype(bf16))
    for h in range(LH):
        tmp[pl.ds(h, TOK, stride=LH), :] = dqp[h]
    oq[...] = tmp[...].reshape(TOK, LH, HEAD_DIM).astype(bf16)

    def last_of(h, state):
        at = pl.ds(h, TOK, stride=LH)
        tk[at, :] = dkp[h] + last_m[...] * nt(vh[h], state)
        tv[at, :] = dvp[h] + last_m[...] * nn(kh[h], state)

    def own_last(g):
        own = split(GROUPS + g, 1, hodd[g], keep_odd).astype(bf16)
        for core in range(2):

            @pl.when(c == core)
            def _(core=core):
                for r in range(GH):
                    last_of(core * HALF + g * GH + r, own[r * HEAD_DIM : (r + 1) * HEAD_DIM])

    def other_last(g):
        i = GROUPS + g

        @pl.when(jnp.logical_or(c == 0, m >= EARLY))
        def _():
            pair_copy(snd.at[i], stb.at[i], back_s.at[i], back_r.at[i]).wait_recv()

        @pl.when(jnp.logical_and(c == 1, m < EARLY))
        def _():
            bytes_of(direct.at[g], CHIPS, dir_r.at[g])
            stb[i] = direct[g].reshape(ROWS, HEAD_DIM)

        for core in range(2):

            @pl.when(oc == core)
            def _(core=core):
                for r in range(GH):
                    last_of(core * HALF + g * GH + r, stb[i, rows_of(r)].astype(bf16))

    own_last(0)
    own_last(1)
    other_last(0)
    other_last(1)

    bytes_of(xb, len(peers), x_s)
    for swap in swaps:
        swap.wait_send()
    for g in range(GROUPS):
        firsts[g].wait_send()
        gives[g].wait_send()
    for g in range(GROUPS):
        pair_copy(snd.at[g], stb.at[g], back_s.at[g], back_r.at[g]).wait_send()

        @pl.when(c == 0)
        def _(g=g):
            bytes_of(direct.at[g], EARLY, dir_s.at[g])

        @pl.when(jnp.logical_or(c == 1, m >= EARLY))
        def _(i=GROUPS + g):
            pair_copy(snd.at[i], stb.at[i], back_s.at[i], back_r.at[i]).wait_send()

    for i in range(2 * GROUPS):
        bytes_of(fr.at[i], CHIPS - 1, fwd_s.at[i])
        bytes_of(sbuf.at[i], CHIPS - 1, ret_s.at[i])


def finish(oq, tk, tv, out_q, out_k, out_v, buf, sem):
    pltpu.make_async_copy(oq, out_q, sem.at[0]).start()
    for n, (src, dst) in enumerate(((tk, out_k), (tv, out_v))):
        for p in range(PIECES):
            rows = pl.ds(p * TOK // PIECES, TOK // PIECES)
            flat = pl.ds(p * TOK * LH // PIECES, TOK * LH // PIECES)
            buf[n, rows] = src[flat, :].reshape(TOK // PIECES, LH, HEAD_DIM).astype(bf16)
            pltpu.make_async_copy(buf.at[n, rows], dst.at[rows], sem.at[1 + n * PIECES + p]).start()
    pltpu.make_async_copy(oq, out_q, sem.at[0]).wait()
    for n, dst in enumerate((out_k, out_v)):
        for p in range(PIECES):
            rows = pl.ds(p * TOK // PIECES, TOK // PIECES)
            pltpu.make_async_copy(buf.at[n, rows], dst.at[rows], sem.at[1 + n * PIECES + p]).wait()


def local(queries, keys, values, out_grad, gain, starts):
    vm = pl.BlockSpec(memory_space=pltpu.VMEM)
    hb = pl.BlockSpec(memory_space=pltpu.HBM)
    args = [
        pltpu.with_memory_space_constraint(a, pltpu.HBM)
        for a in (starts, gain, queries, keys, values, out_grad)
    ]
    flat = jax.ShapeDtypeStruct((TOK * LH, HEAD_DIM), f32)
    out = jax.ShapeDtypeStruct((TOK, LH, HEAD_DIM), bf16)
    V = pltpu.VMEM
    D = pltpu.SemaphoreType.DMA
    N = 2 * GROUPS
    heads16 = V((LH, TOK, HEAD_DIM), bf16)
    heads32 = V((LH, TOK, HEAD_DIM), f32)
    cols = V((TOK, HEAD_DIM), f32)
    half32 = V((HALF, TOK, HEAD_DIM), f32)
    both32 = V((2, HALF, TOK, HEAD_DIM), f32)
    part = V((GROUPS, ROWS, HEAD_DIM), f32)
    parts2 = V((N, ROWS, HEAD_DIM), f32)
    slices = V((N, CHIPS, SL, HEAD_DIM), f32)
    parts = pl.pallas_call(
        kernel,
        out_shape=(out, flat, flat),
        in_specs=[hb] * 6,
        out_specs=(vm, vm, vm),
        scratch_shapes=[
            pltpu.SMEM((4,), jnp.int32),
            V((LH, HEAD_DIM), f32),
            V((4, TOK, LH, HEAD_DIM), bf16),
            V((TOK * LH, HEAD_DIM), f32),
            heads16,
            heads16,
            heads16,
            heads32,
            V((TOK, TOK), f32),
            V((TOK, TOK), f32),
            cols,
            cols,
            V((LH, TOK, TOK), bf16),
            heads16,
            heads32,
            heads32,
            heads32,
            both32,
            both32,
            both32,
            half32,
            half32,
            half32,
            half32,
            V((GROUPS, GH, TOK, HEAD_DIM), f32),
            V((GROUPS, GH, TOK, HEAD_DIM), f32),
            V((2, HALF, TOK, HEAD_DIM), bf16),
            V((2, HALF, HEAD_DIM, TOK), bf16),
            V((2, HALF, HEAD_DIM, HEAD_DIM), bf16),
            V((GROUPS, 2, TOK, HEAD_DIM), f32),
            V((GROUPS, 2, TOK, HEAD_DIM), f32),
            V((2, TOK, HEAD_DIM), f32),
            V((2, TOK, HEAD_DIM), f32),
            V((CHIPS, SL, HEAD_DIM), f32),
            part,
            part,
            part,
            part,
            slices,
            slices,
            slices,
            slices,
            V((GROUPS, CHIPS, SL, HEAD_DIM), f32),
            parts2,
            parts2,
            V((2 * XS, 8, HEAD_DIM), f32),
            V((8, HEAD_DIM), f32),
            D((6,)),
            D((GROUPS,)),
            D((GROUPS,)),
            D((N,)),
            D((N,)),
            D((N,)),
            D((N,)),
            D((GROUPS,)),
            D((GROUPS,)),
            D((N,)),
            D((N,)),
            D((3,)),
            D((3,)),
            D((GROUPS,)),
            D((GROUPS,)),
            D,
            D,
            pltpu.SemaphoreType.REGULAR,
            pltpu.SemaphoreType.REGULAR,
        ],
        compiler_params=pltpu.CompilerParams(
            collective_id=0, has_side_effects=True, vmem_limit_bytes=32 * 2**20
        ),
        cost_estimate=pl.CostEstimate(
            flops=1_400_000_000, bytes_accessed=4_000_000, transcendentals=2048
        ),
        name="fused",
    )(*args)
    return pl.pallas_call(
        finish,
        out_shape=(out, out, out),
        in_specs=[vm] * 3,
        out_specs=(hb, hb, hb),
        scratch_shapes=[V((2, TOK, LH, HEAD_DIM), bf16), D((1 + 2 * PIECES,))],
        compiler_params=pltpu.CompilerParams(vmem_limit_bytes=4 * 2**20),
        name="finish",
    )(*parts)


def solution(mesh):
    spec = P("ctx", "head", None)
    return jax.shard_map(
        local,
        mesh=mesh,
        in_specs=(spec, spec, spec, spec, P("head", None), P()),
        out_specs=(spec, spec, spec),
        check_vma=False,
    )
```
